512 devices in a mesh: dp: 64 (over y, x, z_hi, core), mp: 8 (over z_lo).
Axes of the slice: x: 4, y: 4, z: 16 (z_hi: 2, z_lo: 8; z = z_hi * 8 + z_lo), core: 2. Of those that a mesh axis runs over, the one named last changes fastest.
Arguments:
- activations: bfloat16 [8192, 4096], P('dp', 'mp'), may hold values from -27 to 27
- out_grads: bfloat16 [8192, 8192], P('dp', 'mp'), may hold values from -27 to 27
- grad_weight: bfloat16 [8192, 4096], P('mp', 'dp'), may hold values from -6 to 6
- basis_a: bfloat16 [4096, 512], P('mp'), may hold values from -0.25 to 0.25
- basis_g: bfloat16 [8192, 512], P('mp'), may hold values from -0.25 to 0.25
Outputs:
- factor_a: float32 [4096, 512], P(('mp', 'dp'))
- factor_g: float32 [8192, 512], P(('mp', 'dp'))
- precond: float32 [8192, 4096], P('mp', 'dp')
The draws below stay inside these ranges and needn't reach their ends.
All inputs are finite; a program needn't handle non-finite values.
Results may differ from the reference program's by a relative error of at most 0.0065.
Values may be sent and summed in bfloat16 or wider, within the bound.
A program may use at most 64 MiB of HBM per device.

```python
import jax
import jax.numpy as jnp
from jax import lax

D = 4096
FF = 8192
BLOCK = 512
TOKENS = 8192


def draw_activations(key, part):
    key = jax.random.fold_in(key, 11)
    first, second, third = jax.random.split(key, 3)
    col_scale = jnp.exp(jax.random.uniform(first, (1, D), minval=-1.0, maxval=1.0))
    own_part = jnp.clip(jax.random.normal(second, (TOKENS, D // 32, 32)), -4.0, 4.0)
    shared = 0.6 * jnp.clip(jax.random.normal(third, (TOKENS, D // 32, 1)), -4.0, 4.0)
    mixed = (own_part + shared).reshape(TOKENS, D)
    row_scale = 1.0 + 2.0 * jnp.arange(TOKENS, dtype=jnp.float32)[:, None] / TOKENS
    return (0.5 * mixed * row_scale * col_scale).astype(jnp.bfloat16)


def draw_out_grads(key, part):
    key = jax.random.fold_in(key, 12)
    first, second, third = jax.random.split(key, 3)
    col_scale = jnp.exp(jax.random.uniform(first, (1, FF), minval=-1.0, maxval=1.0))
    own_part = jnp.clip(jax.random.normal(second, (TOKENS, FF // 32, 32)), -4.0, 4.0)
    shared = 0.6 * jnp.clip(jax.random.normal(third, (TOKENS, FF // 32, 1)), -4.0, 4.0)
    mixed = (own_part + shared).reshape(TOKENS, FF)
    row_scale = 3.0 - 2.0 * jnp.arange(TOKENS, dtype=jnp.float32)[:, None] / TOKENS
    return (0.5 * mixed * row_scale * col_scale).astype(jnp.bfloat16)


def block_levels(stream_key, extent, cuts, least, high):
    loudness = 1.0
    for position, shards_of in cuts:
        steps = jax.random.uniform(jax.random.fold_in(jax.random.fold_in(stream_key, 6), position), (shards_of,), jnp.float32, least / len(cuts), high / len(cuts))
        loudness = loudness * jnp.repeat(jnp.exp(steps), extent[position] // shards_of).reshape((-1,) + (1,) * (len(extent) - 1 - position))
    return loudness


def gaussian(rng, shape, width, reach, cuts=(), held_as=jnp.bfloat16):
    loudness = block_levels(rng, shape, cuts, -0.22, 0.18) if cuts else 1.0
    values = jax.random.normal(rng, shape, jnp.float32) * width * loudness
    return jnp.minimum(jnp.maximum(values, -reach), reach).astype(held_as)


def setup_inputs(seed: int = 0) -> dict:
    keys = jax.random.split(jax.random.key(seed), 6)
    activations = draw_activations(jax.random.fold_in(keys[5], 71), 0)
    out_grads = draw_out_grads(jax.random.fold_in(keys[5], 71), 0)
    grad_weight = gaussian(keys[2], (FF, D), 1.0, 6.0, ((0, 8), (1, 64)))
    basis_a = gaussian(keys[3], (D, BLOCK), BLOCK ** -0.5, 0.25, ((0, 8),))
    basis_g = gaussian(keys[4], (FF, BLOCK), BLOCK ** -0.5, 0.25, ((0, 8),))
    return {"activations": activations, "out_grads": out_grads, "grad_weight": grad_weight, "basis_a": basis_a, "basis_g": basis_g}


damping = 0.01


def covariance(values):
    stacked = []
    for number in range(values.shape[1] // BLOCK):
        sliced = values[:, number * BLOCK:(number + 1) * BLOCK].astype(jnp.float32)
        stacked.append(jnp.dot(sliced.T, sliced, preferred_element_type=jnp.float32) / TOKENS)
    return jnp.concatenate(stacked, axis=0)


def projected(factor, basis):
    count = factor.shape[0] // BLOCK
    factor_blocks = factor.reshape(count, BLOCK, BLOCK)
    basis_blocks = basis.astype(jnp.float32).reshape(count, BLOCK, BLOCK)
    product = jnp.einsum("nrs,nsc->nrc", factor_blocks, basis_blocks, precision=lax.Precision.HIGHEST)
    return jnp.sum(basis_blocks * product, axis=1).reshape(-1)


def reference(activations, out_grads, grad_weight, basis_a, basis_g):
    factor_a = covariance(activations)
    factor_g = covariance(out_grads)
    diag_a = projected(factor_a, basis_a)
    diag_g = projected(factor_g, basis_g)
    count_g = FF // BLOCK
    count_a = D // BLOCK
    left_basis = basis_g.astype(jnp.float32).reshape(count_g, BLOCK, BLOCK)
    right_basis = basis_a.astype(jnp.float32).reshape(count_a, BLOCK, BLOCK)
    grad_blocks = grad_weight.astype(jnp.float32).reshape(count_g, BLOCK, D)
    left = jnp.einsum("brs,brd->bsd", left_basis, grad_blocks).astype(jnp.bfloat16).reshape(FF, D)
    left_cols = left.astype(jnp.float32).reshape(FF, count_a, BLOCK)
    rotated = jnp.einsum("rbs,bsc->rbc", left_cols, right_basis).reshape(FF, D)
    scaled = (rotated / (diag_g[:, None] * diag_a[None, :] + damping)).astype(jnp.bfloat16)
    scaled_cols = scaled.astype(jnp.float32).reshape(FF, count_a, BLOCK)
    back = jnp.einsum("rbc,bsc->rbs", scaled_cols, right_basis).astype(jnp.bfloat16).reshape(FF, D)
    back_rows = back.astype(jnp.float32).reshape(count_g, BLOCK, D)
    precond = jnp.einsum("brs,bsd->brd", left_basis, back_rows).reshape(FF, D)
    return factor_a, factor_g, precond
```

```python
import functools

import jax
import jax.numpy as jnp
from jax import lax
from jax.experimental import pallas as pl
from jax.experimental.pallas import tpu as pltpu
from jax.sharding import PartitionSpec as P

MESH = pl.DeviceIdType.MESH
damping = 0.01
CHUNKS = 8


def dot(a, b, dim_a, dim_b):
    return lax.dot_general(a, b, (((dim_a,), (dim_b,)), ((), ())), preferred_element_type=jnp.float32)


def row_picker(size, group, core):
    row = lax.broadcasted_iota(jnp.int32, (size, size // 2), 0)
    col = lax.broadcasted_iota(jnp.int32, (size, size // 2), 1)
    within = lax.rem(col, group)
    return jnp.where(row == (col - within) * 2 + group * core + within, 1.0, 0.0).astype(jnp.bfloat16)


def kernel(
    ny, nx, tokens,
    xa_in, xg_in, w_in, qa_in, pg_in,
    oa_out, og_out, op_out,
    xa, xg, w, qa, pg,
    lsend, lrecv, bsend, brecv,
    dsend, drecv, dzsend, dzrecv, gsend, grecv,
    fsend, frecv, fsum, fzsend, fzrecv,
    oa, og, op,
    load_sem, core_send, core_recv,
    lsend_sem, lrecv_sem, bsend_sem, brecv_sem,
    dsend_sem, drecv_sem, dz_sem, gsend_sem, grecv_sem,
    fsend_sem, frecv_sem, fz_sem, out_sem,
):
    d = lax.axis_index("dp")
    m = lax.axis_index("mp")
    core = lax.rem(d, 2)
    zh = lax.rem(d // 2, 2)
    place = d // 4
    x = lax.rem(place, nx)
    y = place // nx
    places = ny * nx
    group = d // CHUNKS
    lane = lax.rem(d, CHUNKS)
    diagonal = group == m
    rows_a, rows_g = oa.shape[0], og.shape[0]
    block = qa.shape[0]
    cols = w.shape[0]

    twin = (d + 1 - 2 * core, m)
    across = (d + 2 - 4 * zh, m)

    def peer(step, sign):
        dy, dx = step // nx, lax.rem(step, nx)
        to_y = lax.rem(y + sign * dy + ny, ny)
        to_x = lax.rem(x + sign * dx + nx, nx)
        return to_y * nx + to_x

    def at_place(p):
        return (p * 4 + zh * 2 + core, m)

    def friend(q):
        return (m * CHUNKS + q, group)

    def is_me(q):
        return jnp.logical_and(diagonal, q == lane)

    loads = [
        pltpu.make_async_copy(src, dst, load_sem.at[i])
        for i, (src, dst) in enumerate(
            ((w_in, w), (pg_in, pg), (xa_in, xa.at[0]), (xg_in, xg.at[0]), (qa_in, qa))
        )
    ]
    for load in loads:
        load.start()

    barrier = pltpu.get_barrier_semaphore()

    def greet(device):
        pl.semaphore_signal(barrier, inc=1, device_id=device, device_id_type=MESH)

    greet(twin)
    greet(across)

    @pl.loop(1, places)
    def _(step):
        greet(at_place(peer(step, 1)))

    @pl.loop(0, CHUNKS)
    def _(q):
        @pl.when(jnp.logical_not(is_me(q)))
        def _():
            greet(friend(q))

    pl.semaphore_wait(barrier, 2 + places - 1 + CHUNKS - diagonal.astype(jnp.int32))

    swap_a = pltpu.make_async_remote_copy(
        src_ref=xa_in, dst_ref=xa.at[1], send_sem=core_send.at[0], recv_sem=core_recv.at[0],
        device_id=twin, device_id_type=MESH,
    )
    swap_g = pltpu.make_async_remote_copy(
        src_ref=xg_in, dst_ref=xg.at[1], send_sem=core_send.at[1], recv_sem=core_recv.at[1],
        device_id=twin, device_id_type=MESH,
    )
    swap_a.start()
    swap_g.start()

    loads[0].wait()
    loads[1].wait()
    per_block = block // lsend.shape[2]
    for b in range(pg.shape[0] // block):
        left = dot(w[:, b * block:(b + 1) * block], pg[b * block:(b + 1) * block, :], 1, 0)
        left = left.astype(jnp.bfloat16)
        for i in range(per_block):
            lsend[b * per_block + i] = left[:, i * lsend.shape[2]:(i + 1) * lsend.shape[2]]

    def left_copy(q, slot):
        return pltpu.make_async_remote_copy(
            src_ref=lsend.at[q], dst_ref=lrecv.at[slot],
            send_sem=lsend_sem.at[q], recv_sem=lrecv_sem.at[slot],
            device_id=friend(q), device_id_type=MESH,
        )

    def back_copy(q, slot):
        return pltpu.make_async_remote_copy(
            src_ref=bsend.at[q], dst_ref=brecv.at[slot],
            send_sem=bsend_sem.at[q], recv_sem=brecv_sem.at[slot],
            device_id=friend(q), device_id_type=MESH,
        )

    def send_all(copy, src, dst):
        @pl.loop(0, CHUNKS)
        def _(q):
            @pl.when(jnp.logical_not(is_me(q)))
            def _():
                copy(q, lane).start()

            @pl.when(is_me(q))
            def _():
                dst[pl.ds(q, 1)] = src[pl.ds(q, 1)]

    def receive_all(copy):
        @pl.loop(0, CHUNKS)
        def _(k):
            @pl.when(jnp.logical_not(is_me(k)))
            def _():
                copy(k, k).wait_recv()

    def drain_all(copy):
        @pl.loop(0, CHUNKS)
        def _(q):
            @pl.when(jnp.logical_not(is_me(q)))
            def _():
                copy(q, lane).wait_send()

    send_all(left_copy, lsend, lrecv)

    for load in loads[2:]:
        load.wait()
    swap_a.wait_recv()
    swap_g.wait_recv()
    xa_all = xa[...].reshape(-1, block)
    xg_all = [
        xg[:, :, b * block:(b + 1) * block].reshape(-1, block) for b in range(pg.shape[0] // block)
    ]
    half = block // 2
    sides = [(xa_all, qa[...])] + [
        (values, pg[b * block:(b + 1) * block, :]) for b, values in enumerate(xg_all)
    ]
    dsend[...] = jnp.zeros_like(dsend)
    for i, (values, basis) in enumerate(sides):
        turned = dot(values, basis, 1, 0)
        total = jnp.sum(turned * turned, axis=0, keepdims=True)
        dsend[2 * i:2 * i + 1, :] = total[:, :half]
        dsend[2 * i + 1:2 * i + 2, :] = total[:, half:]

    def diag_copy(step):
        return pltpu.make_async_remote_copy(
            src_ref=dsend, dst_ref=drecv.at[step],
            send_sem=dsend_sem.at[step], recv_sem=drecv_sem.at[step],
            device_id=at_place(peer(step, 1)), device_id_type=MESH,
        )

    @pl.loop(1, places)
    def _(step):
        diag_copy(step).start()

    pick_a = row_picker(block, rows_a, core)
    pick_g = row_picker(block, rows_g, core)
    picked = dot(xa_all, pick_a, 1, 0).astype(jnp.bfloat16)
    part = dot(picked, xa_all, 0, 0).astype(jnp.bfloat16)
    fsend[:, 0:2 * rows_a, :] = part.reshape(places, 2 * rows_a, block)
    each = places // len(xg_all)
    for b, values in enumerate(xg_all):
        picked = dot(values, pick_g, 1, 0).astype(jnp.bfloat16)
        part = dot(picked, values, 0, 0).astype(jnp.bfloat16)
        fsend[b * each:(b + 1) * each, 2 * rows_a:, :] = part.reshape(each, 2 * rows_g, block)

    def factor_copy(step):
        to = peer(step, 1)
        return pltpu.make_async_remote_copy(
            src_ref=fsend.at[to], dst_ref=frecv.at[step],
            send_sem=fsend_sem.at[step], recv_sem=frecv_sem.at[step],
            device_id=at_place(to), device_id_type=MESH,
        )

    @pl.loop(1, places)
    def _(step):
        factor_copy(step).start()

    drecv[0] = dsend[...]

    @pl.loop(1, places)
    def _(step):
        diag_copy(step).wait_recv()

    mine = jnp.sum(drecv[...], axis=0)
    dzsend[...] = mine
    for q in range(CHUNKS):
        r, c = 2 + q // 2, (q % 2) * 128
        gsend[q] = jnp.broadcast_to(mine[r:r + 1, c:c + 128], (8, 128))
    dz_copy = pltpu.make_async_remote_copy(
        src_ref=dzsend, dst_ref=dzrecv, send_sem=dz_sem.at[0], recv_sem=dz_sem.at[1],
        device_id=across, device_id_type=MESH,
    )
    dz_copy.start()

    def g_copy(q, slot):
        return pltpu.make_async_remote_copy(
            src_ref=gsend.at[q], dst_ref=grecv.at[slot],
            send_sem=gsend_sem.at[slot], recv_sem=grecv_sem.at[slot],
            device_id=friend(q), device_id_type=MESH,
        )

    other = lane + 2 - 4 * zh
    g_copy(other, 1).start()

    @pl.when(jnp.logical_not(diagonal))
    def _():
        g_copy(lane, 0).start()

    @pl.when(diagonal)
    def _():
        grecv[pl.ds(0, 1)] = gsend[pl.ds(lane, 1)]

    receive_all(left_copy)
    rows = lrecv.shape[2]
    rotated = dot(lrecv[...].reshape(block, rows), qa[...], 0, 0)

    dz_copy.wait_recv()
    g_copy(other, 1).wait_recv()

    @pl.when(jnp.logical_not(diagonal))
    def _():
        g_copy(lane, 0).wait_recv()

    both = (dzsend[0:2, :] + dzrecv[0:2, :]) * (1.0 / tokens)
    diag_a = jnp.concatenate([both[0:1, :], both[1:2, :]], axis=1)
    diag_g = (grecv[0] + grecv[1])[0:1, :] * (1.0 / tokens)
    diag_g = jnp.broadcast_to(diag_g, (rows, rows)).T
    diag_g = jnp.concatenate([diag_g] * (block // rows), axis=1)
    scaled = (rotated / (diag_g * diag_a + damping)).astype(jnp.bfloat16)
    back = dot(qa[...], scaled, 1, 1).astype(jnp.bfloat16)
    bsend[...] = back.reshape(bsend.shape)
    send_all(back_copy, bsend, brecv)

    @pl.loop(1, places)
    def _(step):
        factor_copy(step).wait_recv()

    total = fsend[place].astype(jnp.float32)
    for step in range(1, places):
        total = total + frecv[step].astype(jnp.float32)
    fsum[...] = total
    away_a = fsum[pl.ds(pl.multiple_of((1 - zh) * rows_a, 8), rows_a), :]
    away_g = fsum[pl.ds(pl.multiple_of(2 * rows_a + (1 - zh) * rows_g, 8), rows_g), :]
    fzsend[0:2 * rows_a, :] = jnp.concatenate([away_a[:, :half], away_a[:, half:]], axis=0).astype(jnp.bfloat16)
    fzsend[2 * rows_a:, :] = jnp.concatenate([away_g[:, :half], away_g[:, half:]], axis=0).astype(jnp.bfloat16)
    fz_copy = pltpu.make_async_remote_copy(
        src_ref=fzsend, dst_ref=fzrecv, send_sem=fz_sem.at[0], recv_sem=fz_sem.at[1],
        device_id=across, device_id_type=MESH,
    )
    fz_copy.start()

    receive_all(back_copy)
    for b in range(pg.shape[0] // block):
        lot = jnp.concatenate([brecv[b * per_block + i] for i in range(per_block)], axis=1)
        op[:, b * block:(b + 1) * block] = dot(lot, pg[b * block:(b + 1) * block, :], 1, 1)
    out_p = pltpu.make_async_copy(op, op_out, out_sem.at[0])
    out_p.start()

    fz_copy.wait_recv()
    here_a = fsum[pl.ds(pl.multiple_of(zh * rows_a, 8), rows_a), :]
    here_g = fsum[pl.ds(pl.multiple_of(2 * rows_a + zh * rows_g, 8), rows_g), :]
    there = fzrecv[...].astype(jnp.float32)
    there_a = jnp.concatenate([there[:rows_a], there[rows_a:2 * rows_a]], axis=1)
    there_g = jnp.concatenate([there[2 * rows_a:2 * rows_a + rows_g], there[2 * rows_a + rows_g:]], axis=1)
    oa[...] = (here_a + there_a) * (1.0 / tokens)
    og[...] = (here_g + there_g) * (1.0 / tokens)
    out_a = pltpu.make_async_copy(oa, oa_out, out_sem.at[1])
    out_g = pltpu.make_async_copy(og, og_out, out_sem.at[2])
    out_a.start()
    out_g.start()

    swap_a.wait_send()
    swap_g.wait_send()
    drain_all(left_copy)
    drain_all(back_copy)

    @pl.loop(1, places)
    def _(step):
        diag_copy(step).wait_send()
        factor_copy(step).wait_send()

    dz_copy.wait_send()
    g_copy(other, 1).wait_send()

    @pl.when(jnp.logical_not(diagonal))
    def _():
        g_copy(lane, 0).wait_send()

    fz_copy.wait_send()
    out_p.wait()
    out_a.wait()
    out_g.wait()


def shards(ny, nx, activations, out_grads, grad_weight, basis_a, basis_g):
    replicas = lax.axis_size("dp")
    here, block = activations.shape
    tokens = here * replicas
    wide = out_grads.shape[1]
    rows, cols = grad_weight.shape
    rows_a, rows_g = block // replicas, wide // replicas
    places = ny * nx
    chunk = rows // CHUNKS
    bf16, f32 = jnp.bfloat16, jnp.float32
    dma = pltpu.SemaphoreType.DMA
    vmem = pltpu.VMEM
    scratch = [
        vmem((2, here, block), bf16), vmem((2, here, wide), bf16), vmem((cols, rows), bf16),
        vmem((block, block), bf16), vmem((wide, block), bf16),
        vmem((CHUNKS, cols, chunk), bf16), vmem((CHUNKS, cols, chunk), bf16),
        vmem((CHUNKS, cols, chunk), bf16), vmem((CHUNKS, cols, chunk), bf16),
        vmem((8, block // 2), f32), vmem((places, 8, block // 2), f32),
        vmem((8, block // 2), f32), vmem((8, block // 2), f32),
        vmem((CHUNKS, 8, 128), f32), vmem((2, 8, 128), f32),
        vmem((places, 2 * rows_a + 2 * rows_g, block), bf16),
        vmem((places, 2 * rows_a + 2 * rows_g, block), bf16),
        vmem((2 * rows_a + 2 * rows_g, block), f32),
        vmem((2 * rows_a + 2 * rows_g, block // 2), bf16),
        vmem((2 * rows_a + 2 * rows_g, block // 2), bf16),
        vmem((rows_a, block), f32), vmem((rows_g, block), f32), vmem((cols, rows), f32),
        dma((5,)), dma((2,)), dma((2,)),
        dma((CHUNKS,)), dma((CHUNKS,)), dma((CHUNKS,)), dma((CHUNKS,)),
        dma((places,)), dma((places,)), dma((2,)), dma((2,)), dma((2,)),
        dma((places,)), dma((places,)), dma((2,)), dma((3,)),
    ]
    anywhere = pl.BlockSpec(memory_space=pl.ANY)
    factor_a, factor_g, precond = pl.pallas_call(
        functools.partial(kernel, ny, nx, tokens),
        out_shape=(
            jax.ShapeDtypeStruct((rows_a, block), f32),
            jax.ShapeDtypeStruct((rows_g, block), f32),
            jax.ShapeDtypeStruct((cols, rows), f32),
        ),
        in_specs=[anywhere] * 5,
        out_specs=(anywhere,) * 3,
        scratch_shapes=scratch,
        compiler_params=pltpu.CompilerParams(
            collective_id=0, has_side_effects=True, vmem_limit_bytes=40 * 1024 * 1024
        ),
    )(activations, out_grads, grad_weight.T, basis_a, basis_g)
    return factor_a, factor_g, precond.T


def solution(mesh):
    side = {64: 4, 16: 2}[mesh.shape["dp"]]
    in_specs = (P("dp", "mp"), P("dp", "mp"), P("mp", "dp"), P("mp", None), P("mp", None))
    out_specs = (P(("mp", "dp"), None), P(("mp", "dp"), None), P("mp", "dp"))
    return jax.shard_map(
        functools.partial(shards, side, side), mesh=mesh, in_specs=in_specs, out_specs=out_specs, check_vma=False
    )
```

```python
import functools

import jax
import jax.numpy as jnp
from jax import lax
from jax.experimental import pallas as pl
from jax.experimental.pallas import tpu as pltpu
from jax.sharding import PartitionSpec as P

MESH = pl.DeviceIdType.MESH
damping = 0.01
CHUNKS = 8


def dot(a, b, dim_a, dim_b):
    return lax.dot_general(a, b, (((dim_a,), (dim_b,)), ((), ())), preferred_element_type=jnp.float32)


def row_picker(size, group, core):
    row = lax.broadcasted_iota(jnp.int32, (size, size // 2), 0)
    col = lax.broadcasted_iota(jnp.int32, (size, size // 2), 1)
    within = lax.rem(col, group)
    return jnp.where(row == (col - within) * 2 + group * core + within, 1.0, 0.0).astype(jnp.bfloat16)


def kernel(
    ny, nx, levels, tokens,
    xa_in, xg_in, w_in, qa_in, pg_in,
    oa_out, og_out, op_out,
    xa, xg, w, qa, pg, qj,
    lsend, lrecv, bsend, brecv,
    dsend, drecv, dtwin, dsum, grecv, arecv,
    fsend, frecv, fzsend, fzrecv,
    oa, og, op,
    load_sem, core_send, core_recv, q_send, q_recv, twin_sem,
    lsend_sem, lrecv_sem, bsend_sem, brecv_sem,
    dsend_sem, drecv_sem, gsend_sem, grecv_sem, asend_sem, arecv_sem, dtwin_sem, answer_across, answer_column,
    fsend_sem, frecv_sem, fz_sem, out_sem,
):
    d = lax.axis_index("dp")
    m = lax.axis_index("mp")
    core = lax.rem(d, 2)
    zh = lax.rem(d // 2, 2)
    place = d // 4
    x = lax.rem(place, nx)
    y = place // nx
    places = ny * nx
    group = d // CHUNKS
    lane = lax.rem(d, CHUNKS)
    z = zh * levels + m
    source = group == m
    reach = levels // 2
    spread = nx // 2
    gives = lax.rem(m, spread) == x // 2
    given_y = m // spread
    odd = lax.rem(y, 2)
    late = zh == 1
    facing = lax.rem(m + reach, levels)
    rows_a, rows_g = oa.shape[0], og.shape[0]
    block = qa.shape[0]
    cols = w.shape[0]

    twin = (d + 1 - 2 * core, m)
    across = (d + 2 - 4 * zh, m)

    def peer(step, sign):
        dy, dx = step // nx, lax.rem(step, nx)
        to_y = lax.rem(y + sign * dy + ny, ny)
        to_x = lax.rem(x + sign * dx + nx, nx)
        return to_y * nx + to_x

    def at_place(p):
        return (p * 4 + zh * 2 + core, m)

    def friend(q):
        return (group * CHUNKS + q, facing)

    def at_height(to):
        to = lax.rem(to + 2 * levels, 2 * levels)
        return (place * 4 + (to // levels) * 2 + core, lax.rem(to, levels))

    loads = [
        pltpu.make_async_copy(src, dst, load_sem.at[i])
        for i, (src, dst) in enumerate(
            ((w_in, w), (pg_in, pg), (xa_in, xa.at[0]), (xg_in, xg.at[0]), (qa_in, qa))
        )
    ]
    for load in loads:
        load.start()

    barrier = pltpu.get_barrier_semaphore()

    def greet(device):
        pl.semaphore_signal(barrier, inc=1, device_id=device, device_id_type=MESH)

    greet(twin)

    @pl.loop(1, places)
    def _(step):
        greet(at_place(peer(step, 1)))

    @pl.loop(0, CHUNKS)
    def _(q):
        greet(friend(q))

    def at_yz(to_y, to):
        to = lax.rem(to + 2 * levels, 2 * levels)
        return ((to_y * nx + x) * 4 + (to // levels) * 2 + core, lax.rem(to, levels))

    above = lax.rem(m - group + levels, levels)

    def giver_level(from_y):
        up = jnp.logical_or(above < reach, jnp.logical_and(above == reach, lax.rem(from_y, 2) == 0))
        return jnp.where(up, z - above, z - above + levels)

    for from_y in range(ny):
        @pl.when(jnp.logical_not(jnp.logical_and(source, y == from_y)))
        def _():
            greet(at_yz(from_y, giver_level(from_y)))

    @pl.when(jnp.logical_not(source))
    def _():
        greet(at_height(group + zh * levels))

    @pl.when(jnp.logical_not(late))
    def _():
        greet(across)
        greet(at_height(group + levels))

        @pl.when(source)
        def _():
            @pl.loop(0, levels)
            def _(to):
                greet(at_height(levels + to))

    count = 1 + places - 1 + CHUNKS
    count += jnp.where(gives, levels, 0) - jnp.where(source, 1, 0)
    count += jnp.where(source, levels - 1, 0)
    count += jnp.where(late, 2, 0) + jnp.where(jnp.logical_and(source, late), levels, 0)

    loads[0].wait()
    loads[1].wait()
    per_block = block // lsend.shape[2]
    for b in range(pg.shape[0] // block):
        left = dot(w[:, b * block:(b + 1) * block], pg[b * block:(b + 1) * block, :], 1, 0)
        left = left.astype(jnp.bfloat16)
        for i in range(per_block):
            lsend[b * per_block + i] = left[:, i * lsend.shape[2]:(i + 1) * lsend.shape[2]]

    for load in loads[2:]:
        load.wait()
    sides = [(xa[0], qa[...])] + [
        (xg[0, :, b * block:(b + 1) * block], pg[b * block:(b + 1) * block, :])
        for b in range(pg.shape[0] // block)
    ]
    totals = []
    for values, basis in sides:
        turned = dot(values, basis, 1, 0)
        totals.append(jnp.sum(turned * turned, axis=0, keepdims=True))
    strips = [total[:, i * 128:(i + 1) * 128] for total in totals for i in range(block // 128)]
    strips_a, strips_g = strips[:4], strips[4:]
    for side in range(2):
        dsend[side] = jnp.concatenate(strips_g[side * 4:side * 4 + 4] + strips_a, axis=0)

    pl.semaphore_wait(barrier, count)

    @pl.when(late)
    def _():
        pl.semaphore_signal(answer_across, inc=1, device_id=across, device_id_type=MESH)
        pl.semaphore_signal(answer_column, inc=1, device_id=at_height(group), device_id_type=MESH)

    def diag_copy(step):
        to = peer(step, 1)
        return pltpu.make_async_remote_copy(
            src_ref=dsend.at[lax.rem(to, 2)], dst_ref=drecv.at[step],
            send_sem=dsend_sem.at[step], recv_sem=drecv_sem.at[step],
            device_id=at_place(to), device_id_type=MESH,
        )

    @pl.loop(1, places)
    def _(step):
        diag_copy(step).start()

    swap_a = pltpu.make_async_remote_copy(
        src_ref=xa_in, dst_ref=xa.at[1], send_sem=core_send.at[0], recv_sem=core_recv.at[0],
        device_id=twin, device_id_type=MESH,
    )
    swap_g = pltpu.make_async_remote_copy(
        src_ref=xg_in, dst_ref=xg.at[1], send_sem=core_send.at[1], recv_sem=core_recv.at[1],
        device_id=twin, device_id_type=MESH,
    )
    swap_a.start()
    swap_g.start()

    part = block // ny // 2

    def q_copy(step, from_y):
        return pltpu.make_async_remote_copy(
            src_ref=qa.at[pl.ds(pl.multiple_of((y * 2 + core) * part, 16), part)],
            dst_ref=qj.at[from_y, core],
            send_sem=q_send.at[step], recv_sem=q_recv.at[from_y],
            device_id=at_yz(given_y, z + step + 1 - odd - reach), device_id_type=MESH,
        )

    def q_is_own(step):
        return jnp.logical_and(source, step + 1 - odd == reach)

    @pl.when(gives)
    def _():
        @pl.loop(0, levels)
        def _(step):
            @pl.when(jnp.logical_not(q_is_own(step)))
            def _():
                q_copy(step, y).start()

    to_twin = pltpu.make_async_remote_copy(
        src_ref=qj.at[:, core], dst_ref=qj.at[:, core],
        send_sem=twin_sem.at[0], recv_sem=twin_sem.at[1],
        device_id=twin, device_id_type=MESH,
    )

    def left_copy(q, slot):
        return pltpu.make_async_remote_copy(
            src_ref=lsend.at[q], dst_ref=lrecv.at[slot],
            send_sem=lsend_sem.at[q], recv_sem=lrecv_sem.at[slot],
            device_id=friend(q), device_id_type=MESH,
        )

    def back_copy(q, slot):
        return pltpu.make_async_remote_copy(
            src_ref=bsend.at[q], dst_ref=brecv.at[slot],
            send_sem=bsend_sem.at[q], recv_sem=brecv_sem.at[slot],
            device_id=friend(q), device_id_type=MESH,
        )

    def send_all(copy):
        @pl.loop(0, CHUNKS)
        def _(q):
            copy(q, lane).start()

    def receive_all(copy):
        @pl.loop(0, CHUNKS)
        def _(k):
            copy(k, k).wait_recv()

    def drain_all(copy):
        @pl.loop(0, CHUNKS)
        def _(q):
            copy(q, lane).wait_send()

    send_all(left_copy)

    swap_a.wait_recv()
    swap_g.wait_recv()
    xa_all = xa[...].reshape(-1, block)
    xg_all = [
        xg[:, :, b * block:(b + 1) * block].reshape(-1, block) for b in range(pg.shape[0] // block)
    ]
    half = block // 2

    pick_a = row_picker(block, rows_a, core)
    pick_g = row_picker(block, rows_g, core)
    picked = dot(xa_all, pick_a, 1, 0).astype(jnp.bfloat16)
    product = dot(picked, xa_all, 0, 0).reshape(places, 2, rows_a, block)
    product = jnp.concatenate([product[..., :half], product[..., half:]], axis=2).astype(jnp.bfloat16)
    for side in range(2):
        fsend[side, :, :, 0:half] = product[:, side]
    each = places // len(xg_all)
    for b, values in enumerate(xg_all):
        picked = dot(values, pick_g, 1, 0).astype(jnp.bfloat16)
        product = dot(picked, values, 0, 0).astype(jnp.bfloat16).reshape(each, 2, rows_g, block)
        for side in range(2):
            fsend[side, b * each:(b + 1) * each, :, half:] = product[:, side]

    def factor_copy(side, step):
        to = peer(step, 1)
        return pltpu.make_async_remote_copy(
            src_ref=fsend.at[side, to], dst_ref=frecv.at[side, step],
            send_sem=fsend_sem.at[side, step], recv_sem=frecv_sem.at[side, step],
            device_id=at_place(to), device_id_type=MESH,
        )

    for side in (1 - zh, zh):
        @pl.loop(1, places)
        def _(step):
            factor_copy(side, step).start()

    drecv[0] = dsend[lax.rem(x, 2)]

    @pl.loop(1, places)
    def _(step):
        diag_copy(step).wait_recv()

    dtwin[0] = jnp.sum(drecv[...], axis=0)
    d_copy = pltpu.make_async_remote_copy(
        src_ref=dtwin.at[0], dst_ref=dtwin.at[1], send_sem=dtwin_sem.at[0], recv_sem=dtwin_sem.at[1],
        device_id=twin, device_id_type=MESH,
    )
    d_copy.start()
    d_copy.wait_recv()
    dsum[...] = dtwin[0] + dtwin[1]

    def g_copy(side, slot):
        return pltpu.make_async_remote_copy(
            src_ref=dsum, dst_ref=grecv.at[slot],
            send_sem=gsend_sem.at[side], recv_sem=grecv_sem.at[slot],
            device_id=(place * 4 + side * 2 + core, facing), device_id_type=MESH,
        )

    for side in range(2):
        g_copy(side, zh).start()

    def a_copy(step, slot):
        return pltpu.make_async_remote_copy(
            src_ref=dsum, dst_ref=arecv.at[slot],
            send_sem=asend_sem.at[step], recv_sem=arecv_sem.at[slot],
            device_id=at_height(z + step), device_id_type=MESH,
        )

    @pl.when(source)
    def _():
        @pl.when(jnp.logical_not(late))
        def _():
            pl.semaphore_wait(answer_column, levels)

        @pl.loop(1, 2 * levels)
        def _(step):
            a_copy(step, zh).start()

        arecv[pl.ds(zh, 1)] = dsum[...].reshape(1, 8, 128)

    @pl.when(source)
    def _():
        qj[y, core] = qa[pl.ds(pl.multiple_of((y * 2 + core) * part, 16), part), :]

    for from_y in range(ny):
        @pl.when(jnp.logical_not(jnp.logical_and(source, y == from_y)))
        def _():
            q_copy(0, from_y).wait_recv()

    to_twin.start()

    receive_all(left_copy)
    rows = lrecv.shape[2]
    to_twin.wait_recv()
    rotated = dot(lrecv[...].reshape(block, rows), qj[...].reshape(block, block), 0, 0)

    @pl.when(source)
    def _():
        a_copy(1, 1 - zh).wait_recv()

    @pl.when(jnp.logical_not(source))
    def _():
        for slot in range(2):
            a_copy(1, slot).wait_recv()

    for slot in range(2):
        g_copy(0, slot).wait_recv()

    both_a = (arecv[0] + arecv[1]) * (1.0 / tokens)
    diag_a = jnp.concatenate([both_a[4 + i:5 + i, :] for i in range(block // 128)], axis=1)
    both_g = (grecv[0] + grecv[1]) * (1.0 / tokens)
    first = jnp.where(core == 0, both_g[0:1, :], both_g[1:2, :])
    second = jnp.where(core == 0, both_g[2:3, :], both_g[3:4, :])
    diag_g = jnp.where(zh == 0, first, second)
    diag_g = jnp.broadcast_to(diag_g, (rows, rows)).T
    diag_g = jnp.concatenate([diag_g] * (block // rows), axis=1)
    scaled = (rotated / (diag_g * diag_a + damping)).astype(jnp.bfloat16)
    back = dot(qj[...].reshape(block, block), scaled, 1, 1).astype(jnp.bfloat16)
    bsend[...] = back.reshape(bsend.shape)
    send_all(back_copy)

    def plane_sum(side):
        @pl.loop(1, places)
        def _(step):
            factor_copy(side, step).wait_recv()

        total = fsend[side, place].astype(jnp.float32)
        for step in range(1, places):
            total = total + frecv[side, step].astype(jnp.float32)
        return total

    fzsend[...] = plane_sum(1 - zh).astype(jnp.bfloat16)
    fz_copy = pltpu.make_async_remote_copy(
        src_ref=fzsend, dst_ref=fzrecv, send_sem=fz_sem.at[0], recv_sem=fz_sem.at[1],
        device_id=across, device_id_type=MESH,
    )

    @pl.when(jnp.logical_not(late))
    def _():
        pl.semaphore_wait(answer_across, 1)

    fz_copy.start()
    here = plane_sum(zh)

    receive_all(back_copy)
    for b in range(pg.shape[0] // block):
        lot = jnp.concatenate([brecv[b * per_block + i] for i in range(per_block)], axis=1)
        op[:, b * block:(b + 1) * block] = dot(lot, pg[b * block:(b + 1) * block, :], 1, 1)
    out_p = pltpu.make_async_copy(op, op_out, out_sem.at[0])
    out_p.start()

    fz_copy.wait_recv()
    both = (here + fzrecv[...].astype(jnp.float32)) * (1.0 / tokens)
    oa[...] = jnp.concatenate([both[:rows_a, :half], both[rows_a:, :half]], axis=1)
    og[...] = both[:, half:]
    out_a = pltpu.make_async_copy(oa, oa_out, out_sem.at[1])
    out_g = pltpu.make_async_copy(og, og_out, out_sem.at[2])
    out_a.start()
    out_g.start()

    swap_a.wait_send()
    swap_g.wait_send()
    drain_all(left_copy)
    drain_all(back_copy)

    @pl.loop(1, places)
    def _(step):
        diag_copy(step).wait_send()
        factor_copy(0, step).wait_send()
        factor_copy(1, step).wait_send()

    for side in range(2):
        g_copy(side, zh).wait_send()

    @pl.when(source)
    def _():
        @pl.loop(1, 2 * levels)
        def _(step):
            a_copy(step, zh).wait_send()

    @pl.when(gives)
    def _():
        @pl.loop(0, levels)
        def _(step):
            @pl.when(jnp.logical_not(q_is_own(step)))
            def _():
                q_copy(step, y).wait_send()

    to_twin.wait_send()
    d_copy.wait_send()
    fz_copy.wait_send()
    out_p.wait()
    out_a.wait()
    out_g.wait()


def shards(ny, nx, activations, out_grads, grad_weight, basis_a, basis_g):
    replicas = lax.axis_size("dp")
    here, block = activations.shape
    tokens = here * replicas
    wide = out_grads.shape[1]
    rows, cols = grad_weight.shape
    rows_a, rows_g = block // replicas, wide // replicas
    places = ny * nx
    levels = lax.axis_size("mp")
    chunk = rows // CHUNKS
    bf16, f32 = jnp.bfloat16, jnp.float32
    dma = pltpu.SemaphoreType.DMA
    vmem = pltpu.VMEM
    scratch = [
        vmem((2, here, block), bf16), vmem((2, here, wide), bf16), vmem((cols, rows), bf16),
        vmem((block, block), bf16), vmem((wide, block), bf16), vmem((ny, 2, block // ny // 2, block), bf16),
        vmem((CHUNKS, cols, chunk), bf16), vmem((CHUNKS, cols, chunk), bf16),
        vmem((CHUNKS, cols, chunk), bf16), vmem((CHUNKS, cols, chunk), bf16),
        vmem((2, 8, 128), f32), vmem((places, 8, 128), f32), vmem((2, 8, 128), f32), vmem((8, 128), f32),
        vmem((2, 8, 128), f32), vmem((2, 8, 128), f32),
        vmem((2, places, rows_g, block + block // 2), bf16),
        vmem((2, places, rows_g, block + block // 2), bf16),
        vmem((rows_g, block + block // 2), bf16),
        vmem((rows_g, block + block // 2), bf16),
        vmem((rows_a, block), f32), vmem((rows_g, block), f32), vmem((cols, rows), f32),
        dma((5,)), dma((2,)), dma((2,)), dma((levels,)), dma((ny,)), dma((2,)),
        dma((CHUNKS,)), dma((CHUNKS,)), dma((CHUNKS,)), dma((CHUNKS,)),
        dma((places,)), dma((places,)), dma((2,)), dma((2,)), dma((2 * levels,)), dma((2,)), dma((2,)),
        pltpu.SemaphoreType.REGULAR, pltpu.SemaphoreType.REGULAR,
        dma((2, places)), dma((2, places)), dma((2,)), dma((3,)),
    ]
    anywhere = pl.BlockSpec(memory_space=pltpu.HBM)
    factor_a, factor_g, precond = pl.pallas_call(
        functools.partial(kernel, ny, nx, levels, tokens),
        out_shape=(
            jax.ShapeDtypeStruct((rows_a, block), f32),
            jax.ShapeDtypeStruct((rows_g, block), f32),
            jax.ShapeDtypeStruct((cols, rows), f32),
        ),
        in_specs=[anywhere] * 5,
        out_specs=(anywhere,) * 3,
        scratch_shapes=scratch,
        compiler_params=pltpu.CompilerParams(
            collective_id=0, has_side_effects=True, vmem_limit_bytes=60 * 1024 * 1024
        ),
    )(activations, out_grads, grad_weight.T, basis_a, basis_g)
    return factor_a, factor_g, precond.T


def solution(mesh):
    side = {64: 4, 16: 2}[mesh.shape["dp"]]
    in_specs = (P("dp", "mp"), P("dp", "mp"), P("mp", "dp"), P("mp", None), P("mp", None))
    out_specs = (P(("mp", "dp"), None), P(("mp", "dp"), None), P("mp", "dp"))
    return jax.shard_map(
        functools.partial(shards, side, side), mesh=mesh, in_specs=in_specs, out_specs=out_specs, check_vma=False
    )
```

```python
import functools

import jax
import jax.numpy as jnp
from jax import lax
from jax.experimental import pallas as pl
from jax.experimental.pallas import tpu as pltpu
from jax.sharding import PartitionSpec as P

MESH = pl.DeviceIdType.MESH
damping = 0.01
CHUNKS = 8


def dot(a, b, dim_a, dim_b):
    return lax.dot_general(a, b, (((dim_a,), (dim_b,)), ((), ())), preferred_element_type=jnp.float32)


def row_picker(size, group, core):
    row = lax.broadcasted_iota(jnp.int32, (size, size // 2), 0)
    col = lax.broadcasted_iota(jnp.int32, (size, size // 2), 1)
    within = lax.rem(col, group)
    return jnp.where(row == (col - within) * 2 + group * core + within, 1.0, 0.0).astype(jnp.bfloat16)


def kernel(
    ny, nx, levels, tokens, rows_a, rows_g,
    xa_in, xg_in, w_in, qa_in, pg_in,
    here_out, fzrecv, brecv,
    xa, xg, w, qa, pg, qj,
    lsend, lrecv, bsend,
    dsend, drecv, dtwin, dsum, grecv, arecv,
    fsend, frecv, fzsend, here,
    load_sem, core_send, core_recv, q_send, q_recv, twin_sem,
    lsend_sem, lrecv_sem, bsend_sem, brecv_sem,
    dsend_sem, drecv_sem, gsend_sem, grecv_sem, asend_sem, arecv_sem, dtwin_sem, answer_across, answer_column,
    fsend_sem, frecv_sem, fz_sem, out_sem,
):
    d = lax.axis_index("dp")
    m = lax.axis_index("mp")
    core = lax.rem(d, 2)
    zh = lax.rem(d // 2, 2)
    place = d // 4
    x = lax.rem(place, nx)
    y = place // nx
    places = ny * nx
    group = d // CHUNKS
    lane = lax.rem(d, CHUNKS)
    z = zh * levels + m
    source = group == m
    reach = levels // 2
    spread = nx // 2
    gives = lax.rem(m, spread) == x // 2
    given_y = m // spread
    odd = core
    late = zh == 1
    facing = lax.rem(m + reach, levels)
    block = qa.shape[0]
    cols = w.shape[0]

    twin = (d + 1 - 2 * core, m)
    across = (d + 2 - 4 * zh, m)

    def peer(step, sign):
        dy, dx = step // nx, lax.rem(step, nx)
        to_y = lax.rem(y + sign * dy + ny, ny)
        to_x = lax.rem(x + sign * dx + nx, nx)
        return to_y * nx + to_x

    def at_place(p):
        return (p * 4 + zh * 2 + core, m)

    def friend(q):
        return (group * CHUNKS + q, facing)

    def at_height(to):
        to = lax.rem(to + 2 * levels, 2 * levels)
        return (place * 4 + (to // levels) * 2 + core, lax.rem(to, levels))

    loads = [
        pltpu.make_async_copy(src, dst, load_sem.at[i])
        for i, (src, dst) in enumerate(
            ((w_in, w), (pg_in, pg), (xa_in, xa.at[0]), (xg_in, xg.at[0]), (qa_in, qa))
        )
    ]

    barrier = pltpu.get_barrier_semaphore()

    def greet(device):
        pl.semaphore_signal(barrier, inc=1, device_id=device, device_id_type=MESH)

    @pl.when(jnp.logical_not(source))
    def _():
        greet(at_height(group + zh * levels))

    @pl.when(jnp.logical_not(late))
    def _():
        greet(across)
        greet(at_height(group + levels))

        @pl.when(source)
        def _():
            @pl.loop(0, levels)
            def _(to):
                greet(at_height(levels + to))

    def at_yz(to_y, to):
        to = lax.rem(to + 2 * levels, 2 * levels)
        return ((to_y * nx + x) * 4 + (to // levels) * 2 + core, lax.rem(to, levels))

    above = lax.rem(m - group + levels, levels)

    def giver_level(from_y):
        up = jnp.logical_or(above < reach, jnp.logical_and(above == reach, core == 0))
        return jnp.where(up, z - above, z - above + levels)

    for from_y in range(ny):
        @pl.when(jnp.logical_not(jnp.logical_and(source, y == from_y)))
        def _():
            greet(at_yz(from_y, giver_level(from_y)))

    greet(twin)

    @pl.loop(1, places)
    def _(step):
        greet(at_place(peer(step, 1)))

    @pl.loop(0, CHUNKS)
    def _(q):
        greet(friend(q))

    for load in loads:
        load.start()

    count = 1 + places - 1 + CHUNKS
    count += jnp.where(gives, levels, 0) - jnp.where(source, 1, 0)
    count += jnp.where(source, levels - 1, 0)
    count += jnp.where(late, 2, 0) + jnp.where(jnp.logical_and(source, late), levels, 0)

    loads[0].wait()
    loads[1].wait()
    per_block = block // lsend.shape[2]
    for b in range(pg.shape[0] // block):
        left = dot(w[:, b * block:(b + 1) * block], pg[b * block:(b + 1) * block, :], 1, 0)
        left = left.astype(jnp.bfloat16)
        for i in range(per_block):
            lsend[b * per_block + i] = left[:, i * lsend.shape[2]:(i + 1) * lsend.shape[2]]

    for load in loads[2:]:
        load.wait()
    sides = [(xa[0], qa[...])] + [
        (xg[0, :, b * block:(b + 1) * block], pg[b * block:(b + 1) * block, :])
        for b in range(pg.shape[0] // block)
    ]
    totals = []
    for values, basis in sides:
        turned = dot(values, basis, 1, 0)
        totals.append(jnp.sum(turned * turned, axis=0, keepdims=True))
    strips = [total[:, i * 128:(i + 1) * 128] for total in totals for i in range(block // 128)]
    strips_a, strips_g = strips[:4], strips[4:]
    for side in range(2):
        dsend[side] = jnp.concatenate(strips_g[side * 4:side * 4 + 4] + strips_a, axis=0)

    pl.semaphore_wait(barrier, count)

    @pl.when(late)
    def _():
        pl.semaphore_signal(answer_across, inc=1, device_id=across, device_id_type=MESH)
        pl.semaphore_signal(answer_column.at[m], inc=1, device_id=at_height(group), device_id_type=MESH)

    def diag_copy(step):
        to = peer(step, 1)
        return pltpu.make_async_remote_copy(
            src_ref=dsend.at[lax.rem(to, 2)], dst_ref=drecv.at[step],
            send_sem=dsend_sem.at[step], recv_sem=drecv_sem.at[step],
            device_id=at_place(to), device_id_type=MESH,
        )

    @pl.loop(1, places)
    def _(step):
        diag_copy(step).start()

    swap_a = pltpu.make_async_remote_copy(
        src_ref=xa_in, dst_ref=xa.at[1], send_sem=core_send.at[0], recv_sem=core_recv.at[0],
        device_id=twin, device_id_type=MESH,
    )
    swap_g = pltpu.make_async_remote_copy(
        src_ref=xg_in, dst_ref=xg.at[1], send_sem=core_send.at[1], recv_sem=core_recv.at[1],
        device_id=twin, device_id_type=MESH,
    )
    swap_a.start()
    swap_g.start()

    part = block // ny // 2

    def q_copy(step, from_y):
        return pltpu.make_async_remote_copy(
            src_ref=qa.at[pl.ds(pl.multiple_of((y * 2 + core) * part, 16), part)],
            dst_ref=qj.at[from_y, core],
            send_sem=q_send.at[step], recv_sem=q_recv.at[from_y],
            device_id=at_yz(given_y, z + step + 1 - odd - reach), device_id_type=MESH,
        )

    def q_is_own(step):
        return jnp.logical_and(source, step + 1 - odd == reach)

    @pl.when(gives)
    def _():
        @pl.loop(0, levels)
        def _(step):
            @pl.when(jnp.logical_not(q_is_own(step)))
            def _():
                q_copy(step, y).start()

    to_twin = pltpu.make_async_remote_copy(
        src_ref=qj.at[:, core], dst_ref=qj.at[:, core],
        send_sem=twin_sem.at[0], recv_sem=twin_sem.at[1],
        device_id=twin, device_id_type=MESH,
    )

    def left_copy(q, slot):
        return pltpu.make_async_remote_copy(
            src_ref=lsend.at[q], dst_ref=lrecv.at[slot],
            send_sem=lsend_sem.at[q], recv_sem=lrecv_sem.at[slot],
            device_id=friend(q), device_id_type=MESH,
        )

    def back_copy(q, slot):
        return pltpu.make_async_remote_copy(
            src_ref=bsend.at[q], dst_ref=brecv.at[slot],
            send_sem=bsend_sem.at[q], recv_sem=brecv_sem.at[slot],
            device_id=friend(q), device_id_type=MESH,
        )

    def send_all(copy):
        @pl.loop(0, CHUNKS)
        def _(q):
            copy(q, lane).start()

    def receive_all(copy):
        @pl.loop(0, CHUNKS)
        def _(k):
            copy(k, k).wait_recv()

    def drain_all(copy):
        @pl.loop(0, CHUNKS)
        def _(q):
            copy(q, lane).wait_send()


    swap_a.wait_recv()
    swap_g.wait_recv()
    xa_all = xa[...].reshape(-1, block)
    xg_all = [
        xg[:, :, b * block:(b + 1) * block].reshape(-1, block) for b in range(pg.shape[0] // block)
    ]
    half = block // 2

    pick_a = row_picker(block, rows_a, core)
    pick_g = row_picker(block, rows_g, core)
    picked = dot(xa_all, pick_a, 1, 0).astype(jnp.bfloat16)
    product = dot(picked, xa_all, 0, 0).reshape(places, 2, rows_a, block)
    product = jnp.concatenate([product[..., :half], product[..., half:]], axis=2).astype(jnp.bfloat16)
    for side in range(2):
        fsend[side, :, :, 0:half] = product[:, side]
    each = places // len(xg_all)
    for b, values in enumerate(xg_all):
        picked = dot(values, pick_g, 1, 0).astype(jnp.bfloat16)
        product = dot(picked, values, 0, 0).astype(jnp.bfloat16).reshape(each, 2, rows_g, block)
        for side in range(2):
            fsend[side, b * each:(b + 1) * each, :, half:] = product[:, side]

    def factor_copy(side, step):
        to = peer(step, 1)
        return pltpu.make_async_remote_copy(
            src_ref=fsend.at[side, to], dst_ref=frecv.at[side, step],
            send_sem=fsend_sem.at[side, step], recv_sem=frecv_sem.at[side, step],
            device_id=at_place(to), device_id_type=MESH,
        )

    for side in (1 - zh, zh):
        @pl.loop(1, places)
        def _(step):
            factor_copy(side, step).start()

    send_all(left_copy)

    drecv[0] = dsend[lax.rem(x, 2)]

    @pl.loop(1, places)
    def _(step):
        diag_copy(step).wait_recv()

    dtwin[0] = jnp.sum(drecv[...], axis=0)
    d_copy = pltpu.make_async_remote_copy(
        src_ref=dtwin.at[0], dst_ref=dtwin.at[1], send_sem=dtwin_sem.at[0], recv_sem=dtwin_sem.at[1],
        device_id=twin, device_id_type=MESH,
    )
    d_copy.start()
    d_copy.wait_recv()
    dsum[...] = dtwin[0] + dtwin[1]

    def g_copy(side, slot):
        return pltpu.make_async_remote_copy(
            src_ref=dsum, dst_ref=grecv.at[slot],
            send_sem=gsend_sem.at[side], recv_sem=grecv_sem.at[slot],
            device_id=(place * 4 + side * 2 + core, facing), device_id_type=MESH,
        )

    for side in range(2):
        g_copy(side, zh).start()

    def a_copy(step, slot):
        return pltpu.make_async_remote_copy(
            src_ref=dsum, dst_ref=arecv.at[slot],
            send_sem=asend_sem.at[step], recv_sem=arecv_sem.at[slot],
            device_id=at_height(z + step), device_id_type=MESH,
        )

    @pl.when(jnp.logical_and(source, late))
    def _():
        @pl.loop(1, 2 * levels)
        def _(step):
            a_copy(step, zh).start()

    @pl.when(jnp.logical_and(source, jnp.logical_not(late)))
    def _():
        @pl.loop(1, 2 * levels)
        def _(step):
            @pl.when(lax.rem(z + step, 2 * levels) < levels)
            def _():
                a_copy(step, zh).start()

        @pl.loop(1, levels + 1)
        def _(distance):
            @pl.when(z + distance >= levels)
            def _():
                pl.semaphore_wait(answer_column.at[z + distance - levels], 1)
                a_copy(distance, zh).start()

            @pl.when(jnp.logical_and(z < distance, distance < levels))
            def _():
                pl.semaphore_wait(answer_column.at[z - distance + levels], 1)
                a_copy(2 * levels - distance, zh).start()

    @pl.when(source)
    def _():
        arecv[pl.ds(zh, 1)] = dsum[...].reshape(1, 8, 128)

    def plane_sum(side):
        @pl.loop(1, places)
        def _(step):
            factor_copy(side, step).wait_recv()

        total = fsend[side, place].astype(jnp.float32)
        for step in range(1, places):
            total = total + frecv[side, step].astype(jnp.float32)
        return total

    fzsend[...] = plane_sum(1 - zh).astype(jnp.bfloat16)
    fz_copy = pltpu.make_async_remote_copy(
        src_ref=fzsend, dst_ref=fzrecv, send_sem=fz_sem.at[0], recv_sem=fz_sem.at[1],
        device_id=across, device_id_type=MESH,
    )

    @pl.when(jnp.logical_not(late))
    def _():
        pl.semaphore_wait(answer_across, 1)

    fz_copy.start()

    @pl.when(source)
    def _():
        qj[y, core] = qa[pl.ds(pl.multiple_of((y * 2 + core) * part, 16), part), :]

    for from_y in range(ny):
        @pl.when(jnp.logical_not(jnp.logical_and(source, y == from_y)))
        def _():
            q_copy(0, from_y).wait_recv()

    to_twin.start()

    receive_all(left_copy)
    rows = lrecv.shape[2]
    to_twin.wait_recv()
    rotated = dot(lrecv[...].reshape(block, rows), qj[...].reshape(block, block), 0, 0)

    @pl.when(source)
    def _():
        a_copy(1, 1 - zh).wait_recv()

    @pl.when(jnp.logical_not(source))
    def _():
        for slot in range(2):
            a_copy(1, slot).wait_recv()

    for slot in range(2):
        g_copy(0, slot).wait_recv()

    both_a = (arecv[0] + arecv[1]) * (1.0 / tokens)
    diag_a = jnp.concatenate([both_a[4 + i:5 + i, :] for i in range(block // 128)], axis=1)
    both_g = (grecv[0] + grecv[1]) * (1.0 / tokens)
    first = jnp.where(core == 0, both_g[0:1, :], both_g[1:2, :])
    second = jnp.where(core == 0, both_g[2:3, :], both_g[3:4, :])
    diag_g = jnp.where(zh == 0, first, second)
    diag_g = jnp.broadcast_to(diag_g, (rows, rows)).T
    diag_g = jnp.concatenate([diag_g] * (block // rows), axis=1)
    scaled = (rotated / (diag_g * diag_a + damping)).astype(jnp.bfloat16)
    back = dot(qj[...].reshape(block, block), scaled, 1, 1).astype(jnp.bfloat16)
    bsend[...] = back.reshape(bsend.shape)
    send_all(back_copy)

    here[...] = plane_sum(zh)
    out = pltpu.make_async_copy(here, here_out, out_sem.at[0])
    out.start()
    receive_all(back_copy)
    fz_copy.wait_recv()

    swap_a.wait_send()
    swap_g.wait_send()
    drain_all(left_copy)
    drain_all(back_copy)

    @pl.loop(1, places)
    def _(step):
        diag_copy(step).wait_send()
        factor_copy(0, step).wait_send()
        factor_copy(1, step).wait_send()

    for side in range(2):
        g_copy(side, zh).wait_send()

    @pl.when(source)
    def _():
        @pl.loop(1, 2 * levels)
        def _(step):
            a_copy(step, zh).wait_send()

    @pl.when(gives)
    def _():
        @pl.loop(0, levels)
        def _(step):
            @pl.when(jnp.logical_not(q_is_own(step)))
            def _():
                q_copy(step, y).wait_send()

    to_twin.wait_send()
    d_copy.wait_send()
    fz_copy.wait_send()
    out.wait()


def finish(tokens, rows_a, here, there, back, pg, oa, og, op):
    half = here.shape[1] // 3
    block = pg.shape[1]
    per_block = block // back.shape[2]
    both = (here[...] + there[...].astype(jnp.float32)) * (1.0 / tokens)
    oa[...] = jnp.concatenate([both[:rows_a, :half], both[rows_a:, :half]], axis=1)
    og[...] = both[:, half:]
    for b in range(pg.shape[0] // block):
        lot = jnp.concatenate([back[b * per_block + i] for i in range(per_block)], axis=1)
        op[:, b * block:(b + 1) * block] = dot(lot, pg[b * block:(b + 1) * block, :], 1, 1)


def shards(ny, nx, activations, out_grads, grad_weight, basis_a, basis_g):
    replicas = lax.axis_size("dp")
    here, block = activations.shape
    tokens = here * replicas
    wide = out_grads.shape[1]
    rows, cols = grad_weight.shape
    rows_a, rows_g = block // replicas, wide // replicas
    places = ny * nx
    levels = lax.axis_size("mp")
    chunk = rows // CHUNKS
    bf16, f32 = jnp.bfloat16, jnp.float32
    dma = pltpu.SemaphoreType.DMA
    vmem = pltpu.VMEM
    scratch = [
        vmem((2, here, block), bf16), vmem((2, here, wide), bf16), vmem((cols, rows), bf16),
        vmem((block, block), bf16), vmem((wide, block), bf16), vmem((ny, 2, block // ny // 2, block), bf16),
        vmem((CHUNKS, cols, chunk), bf16), vmem((CHUNKS, cols, chunk), bf16), vmem((CHUNKS, cols, chunk), bf16),
        vmem((2, 8, 128), f32), vmem((places, 8, 128), f32), vmem((2, 8, 128), f32), vmem((8, 128), f32),
        vmem((2, 8, 128), f32), vmem((2, 8, 128), f32),
        vmem((2, places, rows_g, block + block // 2), bf16),
        vmem((2, places, rows_g, block + block // 2), bf16),
        vmem((rows_g, block + block // 2), bf16), vmem((rows_g, block + block // 2), f32),
        dma((5,)), dma((2,)), dma((2,)), dma((levels,)), dma((ny,)), dma((2,)),
        dma((CHUNKS,)), dma((CHUNKS,)), dma((CHUNKS,)), dma((CHUNKS,)),
        dma((places,)), dma((places,)), dma((2,)), dma((2,)), dma((2 * levels,)), dma((2,)), dma((2,)),
        pltpu.SemaphoreType.REGULAR, pltpu.SemaphoreType.REGULAR((levels,)),
        dma((2, places)), dma((2, places)), dma((2,)), dma((1,)),
    ]
    anywhere = pl.BlockSpec(memory_space=pltpu.HBM)
    here, there, back = pl.pallas_call(
        functools.partial(kernel, ny, nx, levels, tokens, rows_a, rows_g),
        out_shape=(
            jax.ShapeDtypeStruct((rows_g, block + block // 2), f32),
            jax.ShapeDtypeStruct((rows_g, block + block // 2), bf16),
            jax.ShapeDtypeStruct((CHUNKS, cols, chunk), bf16),
        ),
        in_specs=[anywhere] * 5,
        out_specs=(anywhere,) * 3,
        scratch_shapes=scratch,
        compiler_params=pltpu.CompilerParams(
            collective_id=0, has_side_effects=True, vmem_limit_bytes=60 * 1024 * 1024
        ),
    )(activations, out_grads, grad_weight.T, basis_a, basis_g)
    inside = pl.BlockSpec(memory_space=pltpu.VMEM)
    factor_a, factor_g, precond = pl.pallas_call(
        functools.partial(finish, tokens, rows_a),
        out_shape=(
            jax.ShapeDtypeStruct((rows_a, block), f32),
            jax.ShapeDtypeStruct((rows_g, block), f32),
            jax.ShapeDtypeStruct((cols, rows), f32),
        ),
        in_specs=[inside] * 4,
        out_specs=(inside,) * 3,
        compiler_params=pltpu.CompilerParams(vmem_limit_bytes=60 * 1024 * 1024),
    )(here, there, back, basis_g)
    return factor_a, factor_g, precond.T


def solution(mesh):
    side = {64: 4, 16: 2}[mesh.shape["dp"]]
    in_specs = (P("dp", "mp"), P("dp", "mp"), P("mp", "dp"), P("mp", None), P("mp", None))
    out_specs = (P(("mp", "dp"), None), P(("mp", "dp"), None), P("mp", "dp"))
    return jax.shard_map(
        functools.partial(shards, side, side), mesh=mesh, in_specs=in_specs, out_specs=out_specs, check_vma=False
    )
```

```python
import functools

import jax
import jax.numpy as jnp
from jax import lax
from jax.experimental import pallas as pl
from jax.experimental.pallas import tpu as pltpu
from jax.sharding import PartitionSpec as P

MESH = pl.DeviceIdType.MESH
damping = 0.01
CHUNKS = 8


def dot(a, b, dim_a, dim_b):
    return lax.dot_general(a, b, (((dim_a,), (dim_b,)), ((), ())), preferred_element_type=jnp.float32)


def row_picker(size, group, core):
    row = lax.broadcasted_iota(jnp.int32, (size, size // 2), 0)
    col = lax.broadcasted_iota(jnp.int32, (size, size // 2), 1)
    within = lax.rem(col, group)
    return jnp.where(row == (col - within) * 2 + group * core + within, 1.0, 0.0).astype(jnp.bfloat16)


def kernel(
    ny, nx, levels, tokens, rows_a, rows_g,
    xa_in, xg_in, w_in, qa_in, pg_in,
    here_out, fzrecv, brecv,
    xa, xg, w, qa, pg, qj,
    lsend, lrecv, bsend,
    dsend, drecv, dtwin, dsum, grecv, arecv,
    fsend, frecv, fzsend, here,
    load_sem, core_send, core_recv, q_send, q_recv, twin_sem,
    lsend_sem, lrecv_sem, bsend_sem, brecv_sem,
    dsend_sem, drecv_sem, gsend_sem, grecv_sem, asend_sem, arecv_sem, dtwin_sem, answer_across, answer_column,
    fsend_sem, frecv_sem, fz_sem, out_sem,
):
    d = lax.axis_index("dp")
    m = lax.axis_index("mp")
    core = lax.rem(d, 2)
    zh = lax.rem(d // 2, 2)
    place = d // 4
    x = lax.rem(place, nx)
    y = place // nx
    places = ny * nx
    group = d // CHUNKS
    lane = lax.rem(d, CHUNKS)
    z = zh * levels + m
    source = group == m
    reach = levels // 2
    spread = nx // 2
    gives = lax.rem(m, spread) == x // 2
    given_y = m // spread
    odd = core
    late = zh == 1
    facing = lax.rem(m + reach, levels)
    block = qa.shape[0]
    cols = w.shape[0]

    twin = (d + 1 - 2 * core, m)
    across = (d + 2 - 4 * zh, m)

    def peer(step, sign):
        dy, dx = step // nx, lax.rem(step, nx)
        to_y = lax.rem(y + sign * dy + ny, ny)
        to_x = lax.rem(x + sign * dx + nx, nx)
        return to_y * nx + to_x

    def at_place(p):
        return (p * 4 + zh * 2 + core, m)

    def friend(q):
        return (group * CHUNKS + q, facing)

    def at_height(to):
        to = lax.rem(to + 2 * levels, 2 * levels)
        return (place * 4 + (to // levels) * 2 + core, lax.rem(to, levels))

    loads = [
        pltpu.make_async_copy(src, dst, load_sem.at[i])
        for i, (src, dst) in enumerate(
            ((w_in, w), (pg_in, pg), (xa_in, xa.at[0]), (xg_in, xg.at[0]), (qa_in, qa))
        )
    ]

    barrier = pltpu.get_barrier_semaphore()

    def greet(device):
        pl.semaphore_signal(barrier, inc=1, device_id=device, device_id_type=MESH)

    @pl.when(jnp.logical_not(source))
    def _():
        greet(at_height(group + zh * levels))

    @pl.when(jnp.logical_not(late))
    def _():
        greet(across)
        greet(at_height(group + levels))

        @pl.when(source)
        def _():
            @pl.loop(0, levels)
            def _(to):
                greet(at_height(levels + to))

    def at_yz(to_y, to):
        to = lax.rem(to + 2 * levels, 2 * levels)
        return ((to_y * nx + x) * 4 + (to // levels) * 2 + core, lax.rem(to, levels))

    above = lax.rem(m - group + levels, levels)

    def giver_level(from_y):
        up = jnp.logical_or(above < reach, jnp.logical_and(above == reach, core == 0))
        return jnp.where(up, z - above, z - above + levels)

    for from_y in range(ny):
        @pl.when(jnp.logical_not(jnp.logical_and(source, y == from_y)))
        def _():
            greet(at_yz(from_y, giver_level(from_y)))

    greet(twin)

    @pl.loop(1, places)
    def _(step):
        greet(at_place(peer(step, 1)))

    @pl.loop(0, CHUNKS)
    def _(q):
        greet(friend(q))

    for load in loads:
        load.start()

    count = 1 + places - 1 + CHUNKS
    count += jnp.where(gives, levels, 0) - jnp.where(source, 1, 0)
    count += jnp.where(source, levels - 1, 0)
    count += jnp.where(late, 2, 0) + jnp.where(jnp.logical_and(source, late), levels, 0)

    loads[0].wait()
    loads[1].wait()
    per_block = block // lsend.shape[2]
    for b in range(pg.shape[0] // block):
        left = dot(w[:, b * block:(b + 1) * block], pg[b * block:(b + 1) * block, :], 1, 0)
        left = left.astype(jnp.bfloat16)
        for i in range(per_block):
            lsend[b * per_block + i] = left[:, i * lsend.shape[2]:(i + 1) * lsend.shape[2]]

    for load in loads[2:]:
        load.wait()
    sides = [(xa[0], qa[...])] + [
        (xg[0, :, b * block:(b + 1) * block], pg[b * block:(b + 1) * block, :])
        for b in range(pg.shape[0] // block)
    ]
    totals = []
    for values, basis in sides:
        turned = dot(values, basis, 1, 0)
        totals.append(jnp.sum(turned * turned, axis=0, keepdims=True))
    strips = [total[:, i * 128:(i + 1) * 128] for total in totals for i in range(block // 128)]
    strips_a, strips_g = strips[:4], strips[4:]
    for side in range(2):
        dsend[side] = jnp.concatenate(strips_g[side * 4:side * 4 + 4] + strips_a, axis=0)

    pl.semaphore_wait(barrier, count)

    @pl.when(late)
    def _():
        pl.semaphore_signal(answer_across, inc=1, device_id=across, device_id_type=MESH)
        pl.semaphore_signal(answer_column.at[m], inc=1, device_id=at_height(group), device_id_type=MESH)

    def diag_copy(step):
        to = peer(step, 1)
        return pltpu.make_async_remote_copy(
            src_ref=dsend.at[lax.rem(to, 2)], dst_ref=drecv.at[step],
            send_sem=dsend_sem.at[step], recv_sem=drecv_sem.at[step],
            device_id=at_place(to), device_id_type=MESH,
        )

    part = block // ny // 2

    def q_copy(step, from_y):
        return pltpu.make_async_remote_copy(
            src_ref=qa.at[pl.ds(pl.multiple_of((y * 2 + core) * part, 16), part)],
            dst_ref=qj.at[from_y, core],
            send_sem=q_send.at[step], recv_sem=q_recv.at[from_y],
            device_id=at_yz(given_y, z + step + 1 - odd - reach), device_id_type=MESH,
        )

    def q_is_own(step):
        return jnp.logical_and(source, step + 1 - odd == reach)

    @pl.when(gives)
    def _():
        @pl.loop(0, levels)
        def _(turn):
            step = jnp.where(lax.rem(turn, 2) == 0, levels - 1 - turn // 2, turn // 2)

            @pl.when(jnp.logical_not(q_is_own(step)))
            def _():
                q_copy(step, y).start()

    def to_twin(from_y, core_side):
        return pltpu.make_async_remote_copy(
            src_ref=qj.at[from_y, core_side], dst_ref=qj.at[from_y, core_side],
            send_sem=twin_sem.at[0, from_y], recv_sem=twin_sem.at[1, from_y],
            device_id=twin, device_id_type=MESH,
        )

    def left_copy(q, slot):
        return pltpu.make_async_remote_copy(
            src_ref=lsend.at[q], dst_ref=lrecv.at[slot],
            send_sem=lsend_sem.at[q], recv_sem=lrecv_sem.at[slot],
            device_id=friend(q), device_id_type=MESH,
        )

    def back_copy(q, slot):
        return pltpu.make_async_remote_copy(
            src_ref=bsend.at[q], dst_ref=brecv.at[slot],
            send_sem=bsend_sem.at[q], recv_sem=brecv_sem.at[slot],
            device_id=friend(q), device_id_type=MESH,
        )

    def send_all(copy):
        @pl.loop(0, CHUNKS)
        def _(q):
            copy(q, lane).start()

    def receive_all(copy):
        @pl.loop(0, CHUNKS)
        def _(k):
            copy(k, k).wait_recv()

    def drain_all(copy):
        @pl.loop(0, CHUNKS)
        def _(q):
            copy(q, lane).wait_send()


    @pl.loop(1, places)
    def _(step):
        diag_copy(step).start()

    swap_a = pltpu.make_async_remote_copy(
        src_ref=xa_in, dst_ref=xa.at[1], send_sem=core_send.at[0], recv_sem=core_recv.at[0],
        device_id=twin, device_id_type=MESH,
    )
    swap_g = pltpu.make_async_remote_copy(
        src_ref=xg_in, dst_ref=xg.at[1], send_sem=core_send.at[1], recv_sem=core_recv.at[1],
        device_id=twin, device_id_type=MESH,
    )
    swap_a.start()
    swap_g.start()

    swap_a.wait_recv()
    swap_g.wait_recv()
    xa_all = xa[...].reshape(-1, block)
    xg_all = [
        xg[:, :, b * block:(b + 1) * block].reshape(-1, block) for b in range(pg.shape[0] // block)
    ]
    half = block // 2

    pick_a = row_picker(block, rows_a, core)
    pick_g = row_picker(block, rows_g, core)
    picked = dot(xa_all, pick_a, 1, 0).astype(jnp.bfloat16)
    product = dot(picked, xa_all, 0, 0).reshape(places, 2, rows_a, block)
    product = jnp.concatenate([product[..., :half], product[..., half:]], axis=2).astype(jnp.bfloat16)
    for side in range(2):
        fsend[side, :, :, 0:half] = product[:, side]
    each = places // len(xg_all)
    for b, values in enumerate(xg_all):
        picked = dot(values, pick_g, 1, 0).astype(jnp.bfloat16)
        product = dot(picked, values, 0, 0).astype(jnp.bfloat16).reshape(each, 2, rows_g, block)
        for side in range(2):
            fsend[side, b * each:(b + 1) * each, :, half:] = product[:, side]

    def factor_copy(side, step):
        to = peer(step, 1)
        return pltpu.make_async_remote_copy(
            src_ref=fsend.at[side, to], dst_ref=frecv.at[side, step],
            send_sem=fsend_sem.at[side, step], recv_sem=frecv_sem.at[side, step],
            device_id=at_place(to), device_id_type=MESH,
        )

    for side in (1 - zh, zh):
        @pl.loop(1, places)
        def _(step):
            factor_copy(side, step).start()

    send_all(left_copy)

    drecv[0] = dsend[lax.rem(x, 2)]

    @pl.loop(1, places)
    def _(step):
        diag_copy(step).wait_recv()

    dtwin[0] = jnp.sum(drecv[...], axis=0)
    d_copy = pltpu.make_async_remote_copy(
        src_ref=dtwin.at[0], dst_ref=dtwin.at[1], send_sem=dtwin_sem.at[0], recv_sem=dtwin_sem.at[1],
        device_id=twin, device_id_type=MESH,
    )
    d_copy.start()
    d_copy.wait_recv()
    dsum[...] = dtwin[0] + dtwin[1]

    def g_copy(side, slot):
        return pltpu.make_async_remote_copy(
            src_ref=dsum, dst_ref=grecv.at[slot],
            send_sem=gsend_sem.at[side], recv_sem=grecv_sem.at[slot],
            device_id=(place * 4 + side * 2 + core, facing), device_id_type=MESH,
        )

    for side in range(2):
        g_copy(side, zh).start()

    def a_copy(step, slot):
        return pltpu.make_async_remote_copy(
            src_ref=dsum, dst_ref=arecv.at[slot],
            send_sem=asend_sem.at[step], recv_sem=arecv_sem.at[slot],
            device_id=at_height(z + step), device_id_type=MESH,
        )

    @pl.when(jnp.logical_and(source, late))
    def _():
        @pl.loop(1, 2 * levels)
        def _(step):
            a_copy(step, zh).start()

    @pl.when(jnp.logical_and(source, jnp.logical_not(late)))
    def _():
        @pl.loop(1, 2 * levels)
        def _(step):
            @pl.when(lax.rem(z + step, 2 * levels) < levels)
            def _():
                a_copy(step, zh).start()

        @pl.loop(1, levels + 1)
        def _(distance):
            @pl.when(z + distance >= levels)
            def _():
                pl.semaphore_wait(answer_column.at[z + distance - levels], 1)
                a_copy(distance, zh).start()

            @pl.when(jnp.logical_and(z < distance, distance < levels))
            def _():
                pl.semaphore_wait(answer_column.at[z - distance + levels], 1)
                a_copy(2 * levels - distance, zh).start()

    @pl.when(source)
    def _():
        arecv[pl.ds(zh, 1)] = dsum[...].reshape(1, 8, 128)

    def plane_sum(side):
        @pl.loop(1, places)
        def _(step):
            factor_copy(side, step).wait_recv()

        total = fsend[side, place].astype(jnp.float32)
        for step in range(1, places):
            total = total + frecv[side, step].astype(jnp.float32)
        return total

    fzsend[...] = plane_sum(1 - zh).astype(jnp.bfloat16)
    fz_copy = pltpu.make_async_remote_copy(
        src_ref=fzsend, dst_ref=fzrecv, send_sem=fz_sem.at[0], recv_sem=fz_sem.at[1],
        device_id=across, device_id_type=MESH,
    )

    @pl.when(jnp.logical_not(late))
    def _():
        pl.semaphore_wait(answer_across, 1)

    fz_copy.start()

    @pl.when(source)
    def _():
        qj[y, core] = qa[pl.ds(pl.multiple_of((y * 2 + core) * part, 16), part), :]

    for from_y in range(ny):
        @pl.when(jnp.logical_not(jnp.logical_and(source, y == from_y)))
        def _():
            q_copy(0, from_y).wait_recv()

        to_twin(from_y, core).start()

    receive_all(left_copy)
    rows = lrecv.shape[2]
    for from_y in range(ny):
        to_twin(from_y, 1 - core).wait_recv()
    rotated = dot(lrecv[...].reshape(block, rows), qj[...].reshape(block, block), 0, 0)

    @pl.when(source)
    def _():
        a_copy(1, 1 - zh).wait_recv()

    @pl.when(jnp.logical_not(source))
    def _():
        for slot in range(2):
            a_copy(1, slot).wait_recv()

    for slot in range(2):
        g_copy(0, slot).wait_recv()

    both_a = (arecv[0] + arecv[1]) * (1.0 / tokens)
    diag_a = jnp.concatenate([both_a[4 + i:5 + i, :] for i in range(block // 128)], axis=1)
    both_g = (grecv[0] + grecv[1]) * (1.0 / tokens)
    first = jnp.where(core == 0, both_g[0:1, :], both_g[1:2, :])
    second = jnp.where(core == 0, both_g[2:3, :], both_g[3:4, :])
    diag_g = jnp.where(zh == 0, first, second)
    diag_g = jnp.broadcast_to(diag_g, (rows, rows)).T
    diag_g = jnp.concatenate([diag_g] * (block // rows), axis=1)
    scaled = (rotated / (diag_g * diag_a + damping)).astype(jnp.bfloat16)
    back = dot(qj[...].reshape(block, block), scaled, 1, 1).astype(jnp.bfloat16)
    bsend[...] = back.reshape(bsend.shape)
    send_all(back_copy)

    here[...] = plane_sum(zh)
    out = pltpu.make_async_copy(here, here_out, out_sem.at[0])
    out.start()
    swap_a.wait_send()
    swap_g.wait_send()
    drain_all(left_copy)

    @pl.loop(1, places)
    def _(step):
        diag_copy(step).wait_send()
        factor_copy(0, step).wait_send()
        factor_copy(1, step).wait_send()

    for side in range(2):
        g_copy(side, zh).wait_send()

    @pl.when(source)
    def _():
        @pl.loop(1, 2 * levels)
        def _(step):
            a_copy(step, zh).wait_send()

    @pl.when(gives)
    def _():
        @pl.loop(0, levels)
        def _(step):
            @pl.when(jnp.logical_not(q_is_own(step)))
            def _():
                q_copy(step, y).wait_send()

    for from_y in range(ny):
        to_twin(from_y, core).wait_send()

    d_copy.wait_send()
    fz_copy.wait_send()
    out.wait()

    receive_all(back_copy)
    fz_copy.wait_recv()

    drain_all(back_copy)


def finish(tokens, rows_a, here, there, back, pg, oa, og, op):
    half = here.shape[1] // 3
    block = pg.shape[1]
    per_block = block // back.shape[2]
    both = (here[...] + there[...].astype(jnp.float32)) * (1.0 / tokens)
    oa[...] = jnp.concatenate([both[:rows_a, :half], both[rows_a:, :half]], axis=1)
    og[...] = both[:, half:]
    for b in range(pg.shape[0] // block):
        lot = jnp.concatenate([back[b * per_block + i] for i in range(per_block)], axis=1)
        op[:, b * block:(b + 1) * block] = dot(lot, pg[b * block:(b + 1) * block, :], 1, 1)


def shards(ny, nx, activations, out_grads, grad_weight, basis_a, basis_g):
    replicas = lax.axis_size("dp")
    here, block = activations.shape
    tokens = here * replicas
    wide = out_grads.shape[1]
    rows, cols = grad_weight.shape
    rows_a, rows_g = block // replicas, wide // replicas
    places = ny * nx
    levels = lax.axis_size("mp")
    chunk = rows // CHUNKS
    bf16, f32 = jnp.bfloat16, jnp.float32
    dma = pltpu.SemaphoreType.DMA
    vmem = pltpu.VMEM
    scratch = [
        vmem((2, here, block), bf16), vmem((2, here, wide), bf16), vmem((cols, rows), bf16),
        vmem((block, block), bf16), vmem((wide, block), bf16), vmem((ny, 2, block // ny // 2, block), bf16),
        vmem((CHUNKS, cols, chunk), bf16), vmem((CHUNKS, cols, chunk), bf16), vmem((CHUNKS, cols, chunk), bf16),
        vmem((2, 8, 128), f32), vmem((places, 8, 128), f32), vmem((2, 8, 128), f32), vmem((8, 128), f32),
        vmem((2, 8, 128), f32), vmem((2, 8, 128), f32),
        vmem((2, places, rows_g, block + block // 2), bf16),
        vmem((2, places, rows_g, block + block // 2), bf16),
        vmem((rows_g, block + block // 2), bf16), vmem((rows_g, block + block // 2), f32),
        dma((5,)), dma((2,)), dma((2,)), dma((levels,)), dma((ny,)), dma((2, ny)),
        dma((CHUNKS,)), dma((CHUNKS,)), dma((CHUNKS,)), dma((CHUNKS,)),
        dma((places,)), dma((places,)), dma((2,)), dma((2,)), dma((2 * levels,)), dma((2,)), dma((2,)),
        pltpu.SemaphoreType.REGULAR, pltpu.SemaphoreType.REGULAR((levels,)),
        dma((2, places)), dma((2, places)), dma((2,)), dma((1,)),
    ]
    anywhere = pl.BlockSpec(memory_space=pltpu.HBM)
    here, there, back = pl.pallas_call(
        functools.partial(kernel, ny, nx, levels, tokens, rows_a, rows_g),
        out_shape=(
            jax.ShapeDtypeStruct((rows_g, block + block // 2), f32),
            jax.ShapeDtypeStruct((rows_g, block + block // 2), bf16),
            jax.ShapeDtypeStruct((CHUNKS, cols, chunk), bf16),
        ),
        in_specs=[anywhere] * 5,
        out_specs=(anywhere,) * 3,
        scratch_shapes=scratch,
        compiler_params=pltpu.CompilerParams(
            collective_id=0, has_side_effects=True, vmem_limit_bytes=60 * 1024 * 1024
        ),
    )(activations, out_grads, grad_weight.T, basis_a, basis_g)
    inside = pl.BlockSpec(memory_space=pltpu.VMEM)
    factor_a, factor_g, precond = pl.pallas_call(
        functools.partial(finish, tokens, rows_a),
        out_shape=(
            jax.ShapeDtypeStruct((rows_a, block), f32),
            jax.ShapeDtypeStruct((rows_g, block), f32),
            jax.ShapeDtypeStruct((cols, rows), f32),
        ),
        in_specs=[inside] * 4,
        out_specs=(inside,) * 3,
        compiler_params=pltpu.CompilerParams(vmem_limit_bytes=60 * 1024 * 1024),
    )(here, there, back, basis_g)
    return factor_a, factor_g, precond.T


def solution(mesh):
    side = {64: 4, 16: 2}[mesh.shape["dp"]]
    in_specs = (P("dp", "mp"), P("dp", "mp"), P("mp", "dp"), P("mp", None), P("mp", None))
    out_specs = (P(("mp", "dp"), None), P(("mp", "dp"), None), P("mp", "dp"))
    return jax.shard_map(
        functools.partial(shards, side, side), mesh=mesh, in_specs=in_specs, out_specs=out_specs, check_vma=False
    )
```

```python
import functools

import jax
import jax.numpy as jnp
from jax import lax
from jax.experimental import pallas as pl
from jax.experimental.pallas import tpu as pltpu
from jax.sharding import PartitionSpec as P

MESH = pl.DeviceIdType.MESH
damping = 0.01
CHUNKS = 8


def dot(a, b, dim_a, dim_b):
    return lax.dot_general(a, b, (((dim_a,), (dim_b,)), ((), ())), preferred_element_type=jnp.float32)


def row_picker(size, group, core):
    row = lax.broadcasted_iota(jnp.int32, (size, size // 2), 0)
    col = lax.broadcasted_iota(jnp.int32, (size, size // 2), 1)
    within = lax.rem(col, group)
    return jnp.where(row == (col - within) * 2 + group * core + within, 1.0, 0.0).astype(jnp.bfloat16)


def kernel(
    ny, nx, levels, tokens, rows_a, rows_g,
    xa_in, xg_in, w_in, qa_in, pg_in,
    here_out, fzrecv, brecv,
    xa, xg, w, qa, pg, qj,
    lsend, lrecv, bsend,
    dsend, drecv, dtwin, dsum, grecv, arecv,
    fsend, frecv, fzsend, here,
    load_sem, core_send, core_recv, q_send, q_recv, twin_sem,
    lsend_sem, lrecv_sem, bsend_sem, brecv_sem,
    dsend_sem, drecv_sem, gsend_sem, grecv_sem, asend_sem, arecv_sem, dtwin_sem, answer_across, answer_column,
    fsend_sem, frecv_sem, fz_sem, out_sem,
):
    d = lax.axis_index("dp")
    m = lax.axis_index("mp")
    core = lax.rem(d, 2)
    zh = lax.rem(d // 2, 2)
    place = d // 4
    x = lax.rem(place, nx)
    y = place // nx
    places = ny * nx
    group = d // CHUNKS
    lane = lax.rem(d, CHUNKS)
    z = zh * levels + m
    source = group == m
    reach = levels // 2
    spread = nx // 2
    gives = lax.rem(m, spread) == x // 2
    given_y = m // spread
    odd = core
    late = zh == 1
    facing = lax.rem(m + reach, levels)
    block = qa.shape[0]
    cols = w.shape[0]

    twin = (d + 1 - 2 * core, m)
    across = (d + 2 - 4 * zh, m)

    def peer(step, sign):
        dy, dx = step // nx, lax.rem(step, nx)
        to_y = lax.rem(y + sign * dy + ny, ny)
        to_x = lax.rem(x + sign * dx + nx, nx)
        return to_y * nx + to_x

    def at_place(p):
        return (p * 4 + zh * 2 + core, m)

    def friend(q):
        return (group * CHUNKS + q, facing)

    def at_height(to):
        to = lax.rem(to + 2 * levels, 2 * levels)
        return (place * 4 + (to // levels) * 2 + core, lax.rem(to, levels))

    loads = [
        pltpu.make_async_copy(src, dst, load_sem.at[i])
        for i, (src, dst) in enumerate(
            ((w_in, w), (pg_in, pg), (xa_in, xa.at[0]), (xg_in, xg.at[0]), (qa_in, qa))
        )
    ]

    barrier = pltpu.get_barrier_semaphore()

    def greet(device):
        pl.semaphore_signal(barrier, inc=1, device_id=device, device_id_type=MESH)

    @pl.when(jnp.logical_not(source))
    def _():
        greet(at_height(group + zh * levels))

    @pl.when(jnp.logical_not(late))
    def _():
        greet(across)
        greet(at_height(group + levels))

        @pl.when(source)
        def _():
            @pl.loop(0, levels)
            def _(to):
                greet(at_height(levels + to))

    def at_yz(to_y, to):
        to = lax.rem(to + 2 * levels, 2 * levels)
        return ((to_y * nx + x) * 4 + (to // levels) * 2 + core, lax.rem(to, levels))

    above = lax.rem(m - group + levels, levels)

    def giver_level(from_y):
        up = jnp.logical_or(above < reach, jnp.logical_and(above == reach, core == 0))
        return jnp.where(up, z - above, z - above + levels)

    for from_y in range(ny):
        @pl.when(jnp.logical_not(jnp.logical_and(source, y == from_y)))
        def _():
            greet(at_yz(from_y, giver_level(from_y)))

    greet(twin)

    @pl.loop(1, places)
    def _(step):
        greet(at_place(peer(step, 1)))

    @pl.loop(0, CHUNKS)
    def _(q):
        greet(friend(q))

    for load in loads:
        load.start()

    count = 1 + places - 1 + CHUNKS
    count += jnp.where(gives, levels, 0) - jnp.where(source, 1, 0)
    count += jnp.where(source, levels - 1, 0)
    count += jnp.where(late, 2, 0) + jnp.where(jnp.logical_and(source, late), levels, 0)

    loads[0].wait()
    loads[1].wait()
    per_block = block // lsend.shape[2]
    for b in range(pg.shape[0] // block):
        left = dot(w[:, b * block:(b + 1) * block], pg[b * block:(b + 1) * block, :], 1, 0)
        left = left.astype(jnp.bfloat16)
        for i in range(per_block):
            lsend[b * per_block + i] = left[:, i * lsend.shape[2]:(i + 1) * lsend.shape[2]]

    for load in loads[2:]:
        load.wait()
    sides = [(xa[0], qa[...])] + [
        (xg[0, :, b * block:(b + 1) * block], pg[b * block:(b + 1) * block, :])
        for b in range(pg.shape[0] // block)
    ]
    totals = []
    for values, basis in sides:
        turned = dot(values, basis, 1, 0)
        totals.append(jnp.sum(turned * turned, axis=0, keepdims=True))
    strips = [total[:, i * 128:(i + 1) * 128] for total in totals for i in range(block // 128)]
    strips_a, strips_g = strips[:4], strips[4:]
    for side in range(2):
        dsend[side] = jnp.concatenate(strips_g[side * 4:side * 4 + 4] + strips_a, axis=0)

    pl.semaphore_wait(barrier, count)

    @pl.when(late)
    def _():
        pl.semaphore_signal(answer_across, inc=1, device_id=across, device_id_type=MESH)
        pl.semaphore_signal(answer_column.at[m], inc=1, device_id=at_height(group), device_id_type=MESH)

    def diag_copy(step):
        to = peer(step, 1)
        return pltpu.make_async_remote_copy(
            src_ref=dsend.at[lax.rem(to, 2)], dst_ref=drecv.at[step],
            send_sem=dsend_sem.at[step], recv_sem=drecv_sem.at[step],
            device_id=at_place(to), device_id_type=MESH,
        )

    part = block // ny // 2

    def q_copy(step, from_y):
        return pltpu.make_async_remote_copy(
            src_ref=qa.at[pl.ds(pl.multiple_of((y * 2 + core) * part, 16), part)],
            dst_ref=qj.at[from_y, core],
            send_sem=q_send.at[step], recv_sem=q_recv.at[from_y],
            device_id=at_yz(given_y, z + step + 1 - odd - reach), device_id_type=MESH,
        )

    def q_is_own(step):
        return jnp.logical_and(source, step + 1 - odd == reach)

    @pl.when(gives)
    def _():
        @pl.loop(0, levels)
        def _(turn):
            step = jnp.where(lax.rem(turn, 2) == 0, levels - 1 - turn // 2, turn // 2)

            @pl.when(jnp.logical_not(q_is_own(step)))
            def _():
                q_copy(step, y).start()

    def to_twin(from_y, core_side):
        return pltpu.make_async_remote_copy(
            src_ref=qj.at[from_y, core_side], dst_ref=qj.at[from_y, core_side],
            send_sem=twin_sem.at[0, from_y], recv_sem=twin_sem.at[1, from_y],
            device_id=twin, device_id_type=MESH,
        )

    def left_copy(q, slot):
        return pltpu.make_async_remote_copy(
            src_ref=lsend.at[q], dst_ref=lrecv.at[slot],
            send_sem=lsend_sem.at[q], recv_sem=lrecv_sem.at[slot],
            device_id=friend(q), device_id_type=MESH,
        )

    def back_copy(q, slot):
        return pltpu.make_async_remote_copy(
            src_ref=bsend.at[q], dst_ref=brecv.at[slot],
            send_sem=bsend_sem.at[q], recv_sem=brecv_sem.at[slot],
            device_id=friend(q), device_id_type=MESH,
        )

    def send_all(copy):
        @pl.loop(0, CHUNKS)
        def _(q):
            copy(q, lane).start()

    def receive_all(copy):
        @pl.loop(0, CHUNKS)
        def _(k):
            copy(k, k).wait_recv()

    def drain_all(copy):
        @pl.loop(0, CHUNKS)
        def _(q):
            copy(q, lane).wait_send()


    @pl.loop(1, places)
    def _(step):
        diag_copy(step).start()

    swap_a = pltpu.make_async_remote_copy(
        src_ref=xa_in, dst_ref=xa.at[1], send_sem=core_send.at[0], recv_sem=core_recv.at[0],
        device_id=twin, device_id_type=MESH,
    )
    swap_g = pltpu.make_async_remote_copy(
        src_ref=xg_in, dst_ref=xg.at[1], send_sem=core_send.at[1], recv_sem=core_recv.at[1],
        device_id=twin, device_id_type=MESH,
    )
    swap_a.start()
    swap_g.start()

    swap_a.wait_recv()
    swap_g.wait_recv()
    xa_all = xa[...].reshape(-1, block)
    xg_all = [
        xg[:, :, b * block:(b + 1) * block].reshape(-1, block) for b in range(pg.shape[0] // block)
    ]
    half = block // 2

    pick_a = row_picker(block, rows_a, core)
    pick_g = row_picker(block, rows_g, core)
    picked = dot(xa_all, pick_a, 1, 0).astype(jnp.bfloat16)
    product = dot(picked, xa_all, 0, 0).reshape(places, 2, rows_a, block)
    product = jnp.concatenate([product[..., :half], product[..., half:]], axis=2).astype(jnp.bfloat16)
    for side in range(2):
        fsend[side, :, :, 0:half] = product[:, side]
    each = places // len(xg_all)
    for b, values in enumerate(xg_all):
        picked = dot(values, pick_g, 1, 0).astype(jnp.bfloat16)
        product = dot(picked, values, 0, 0).astype(jnp.bfloat16).reshape(each, 2, rows_g, block)
        for side in range(2):
            fsend[side, b * each:(b + 1) * each, :, half:] = product[:, side]

    def factor_copy(side, step):
        to = peer(step, 1)
        return pltpu.make_async_remote_copy(
            src_ref=fsend.at[side, to], dst_ref=frecv.at[side, step],
            send_sem=fsend_sem.at[side, step], recv_sem=frecv_sem.at[side, step],
            device_id=at_place(to), device_id_type=MESH,
        )

    for side in (1 - zh, zh):
        @pl.loop(1, places)
        def _(step):
            factor_copy(side, step).start()

    send_all(left_copy)

    drecv[0] = dsend[lax.rem(x, 2)]

    @pl.loop(1, places)
    def _(step):
        diag_copy(step).wait_recv()

    dtwin[0] = jnp.sum(drecv[...], axis=0)
    d_copy = pltpu.make_async_remote_copy(
        src_ref=dtwin.at[0], dst_ref=dtwin.at[1], send_sem=dtwin_sem.at[0], recv_sem=dtwin_sem.at[1],
        device_id=twin, device_id_type=MESH,
    )
    d_copy.start()
    d_copy.wait_recv()
    dsum[...] = dtwin[0] + dtwin[1]

    def g_copy(side, slot):
        return pltpu.make_async_remote_copy(
            src_ref=dsum, dst_ref=grecv.at[slot],
            send_sem=gsend_sem.at[side], recv_sem=grecv_sem.at[slot],
            device_id=(place * 4 + side * 2 + core, facing), device_id_type=MESH,
        )

    for side in range(2):
        g_copy(side, zh).start()

    def a_copy(step, slot):
        return pltpu.make_async_remote_copy(
            src_ref=dsum, dst_ref=arecv.at[slot],
            send_sem=asend_sem.at[step], recv_sem=arecv_sem.at[slot],
            device_id=at_height(z + step), device_id_type=MESH,
        )

    @pl.when(jnp.logical_and(source, late))
    def _():
        @pl.loop(1, 2 * levels)
        def _(step):
            a_copy(step, zh).start()

    @pl.when(jnp.logical_and(source, jnp.logical_not(late)))
    def _():
        @pl.loop(1, 2 * levels)
        def _(step):
            @pl.when(lax.rem(z + step, 2 * levels) < levels)
            def _():
                a_copy(step, zh).start()

        @pl.loop(1, levels + 1)
        def _(distance):
            @pl.when(z + distance >= levels)
            def _():
                pl.semaphore_wait(answer_column.at[z + distance - levels], 1)
                a_copy(distance, zh).start()

            @pl.when(jnp.logical_and(z < distance, distance < levels))
            def _():
                pl.semaphore_wait(answer_column.at[z - distance + levels], 1)
                a_copy(2 * levels - distance, zh).start()

    @pl.when(source)
    def _():
        arecv[pl.ds(zh, 1)] = dsum[...].reshape(1, 8, 128)

    def plane_sum(side):
        @pl.loop(1, places)
        def _(step):
            factor_copy(side, step).wait_recv()

        total = fsend[side, place].astype(jnp.float32)
        for step in range(1, places):
            total = total + frecv[side, step].astype(jnp.float32)
        return total

    fzsend[...] = plane_sum(1 - zh).astype(jnp.bfloat16)
    fz_copy = pltpu.make_async_remote_copy(
        src_ref=fzsend, dst_ref=fzrecv, send_sem=fz_sem.at[0], recv_sem=fz_sem.at[1],
        device_id=across, device_id_type=MESH,
    )

    @pl.when(jnp.logical_not(late))
    def _():
        pl.semaphore_wait(answer_across, 1)

    fz_copy.start()

    @pl.when(source)
    def _():
        qj[y, core] = qa[pl.ds(pl.multiple_of((y * 2 + core) * part, 16), part), :]

    for from_y in range(ny):
        @pl.when(jnp.logical_not(jnp.logical_and(source, y == from_y)))
        def _():
            q_copy(0, from_y).wait_recv()

        to_twin(from_y, core).start()

    receive_all(left_copy)
    rows = lrecv.shape[2]
    for from_y in range(ny):
        to_twin(from_y, 1 - core).wait_recv()
    rotated = dot(lrecv[...].reshape(block, rows), qj[...].reshape(block, block), 0, 0)

    @pl.when(source)
    def _():
        a_copy(1, 1 - zh).wait_recv()

    @pl.when(jnp.logical_not(source))
    def _():
        for slot in range(2):
            a_copy(1, slot).wait_recv()

    for slot in range(2):
        g_copy(0, slot).wait_recv()

    both_a = (arecv[0] + arecv[1]) * (1.0 / tokens)
    diag_a = jnp.concatenate([both_a[4 + i:5 + i, :] for i in range(block // 128)], axis=1)
    both_g = (grecv[0] + grecv[1]) * (1.0 / tokens)
    first = jnp.where(core == 0, both_g[0:1, :], both_g[1:2, :])
    second = jnp.where(core == 0, both_g[2:3, :], both_g[3:4, :])
    diag_g = jnp.where(zh == 0, first, second)
    diag_g = jnp.broadcast_to(diag_g, (rows, rows)).T
    diag_g = jnp.concatenate([diag_g] * (block // rows), axis=1)
    scaled = (rotated / (diag_g * diag_a + damping)).astype(jnp.bfloat16)
    back = dot(qj[...].reshape(block, block), scaled, 1, 1).astype(jnp.bfloat16)
    bsend[...] = back.reshape(bsend.shape)
    for side in range(2):
        for q in range(CHUNKS):
            if q // 2 % 2 == side:
                back_copy(q, lane).start()

    here[...] = plane_sum(zh)
    out = pltpu.make_async_copy(here, here_out, out_sem.at[0])
    out.start()
    swap_a.wait_send()
    swap_g.wait_send()
    drain_all(left_copy)

    @pl.loop(1, places)
    def _(step):
        diag_copy(step).wait_send()
        factor_copy(0, step).wait_send()
        factor_copy(1, step).wait_send()

    for side in range(2):
        g_copy(side, zh).wait_send()

    @pl.when(source)
    def _():
        @pl.loop(1, 2 * levels)
        def _(step):
            a_copy(step, zh).wait_send()

    @pl.when(gives)
    def _():
        @pl.loop(0, levels)
        def _(step):
            @pl.when(jnp.logical_not(q_is_own(step)))
            def _():
                q_copy(step, y).wait_send()

    for from_y in range(ny):
        to_twin(from_y, core).wait_send()

    d_copy.wait_send()
    fz_copy.wait_send()
    out.wait()

    receive_all(back_copy)
    fz_copy.wait_recv()

    drain_all(back_copy)


def finish(tokens, rows_a, here, there, back, pg, oa, og, op):
    half = here.shape[1] // 3
    block = pg.shape[1]
    per_block = block // back.shape[2]
    both = (here[...] + there[...].astype(jnp.float32)) * (1.0 / tokens)
    oa[...] = jnp.concatenate([both[:rows_a, :half], both[rows_a:, :half]], axis=1)
    og[...] = both[:, half:]
    for b in range(pg.shape[0] // block):
        lot = jnp.concatenate([back[b * per_block + i] for i in range(per_block)], axis=1)
        op[:, b * block:(b + 1) * block] = dot(lot, pg[b * block:(b + 1) * block, :], 1, 1)


def shards(ny, nx, activations, out_grads, grad_weight, basis_a, basis_g):
    replicas = lax.axis_size("dp")
    here, block = activations.shape
    tokens = here * replicas
    wide = out_grads.shape[1]
    rows, cols = grad_weight.shape
    rows_a, rows_g = block // replicas, wide // replicas
    places = ny * nx
    levels = lax.axis_size("mp")
    chunk = rows // CHUNKS
    bf16, f32 = jnp.bfloat16, jnp.float32
    dma = pltpu.SemaphoreType.DMA
    vmem = pltpu.VMEM
    scratch = [
        vmem((2, here, block), bf16), vmem((2, here, wide), bf16), vmem((cols, rows), bf16),
        vmem((block, block), bf16), vmem((wide, block), bf16), vmem((ny, 2, block // ny // 2, block), bf16),
        vmem((CHUNKS, cols, chunk), bf16), vmem((CHUNKS, cols, chunk), bf16), vmem((CHUNKS, cols, chunk), bf16),
        vmem((2, 8, 128), f32), vmem((places, 8, 128), f32), vmem((2, 8, 128), f32), vmem((8, 128), f32),
        vmem((2, 8, 128), f32), vmem((2, 8, 128), f32),
        vmem((2, places, rows_g, block + block // 2), bf16),
        vmem((2, places, rows_g, block + block // 2), bf16),
        vmem((rows_g, block + block // 2), bf16), vmem((rows_g, block + block // 2), f32),
        dma((5,)), dma((2,)), dma((2,)), dma((levels,)), dma((ny,)), dma((2, ny)),
        dma((CHUNKS,)), dma((CHUNKS,)), dma((CHUNKS,)), dma((CHUNKS,)),
        dma((places,)), dma((places,)), dma((2,)), dma((2,)), dma((2 * levels,)), dma((2,)), dma((2,)),
        pltpu.SemaphoreType.REGULAR, pltpu.SemaphoreType.REGULAR((levels,)),
        dma((2, places)), dma((2, places)), dma((2,)), dma((1,)),
    ]
    anywhere = pl.BlockSpec(memory_space=pltpu.HBM)
    here, there, back = pl.pallas_call(
        functools.partial(kernel, ny, nx, levels, tokens, rows_a, rows_g),
        out_shape=(
            jax.ShapeDtypeStruct((rows_g, block + block // 2), f32),
            jax.ShapeDtypeStruct((rows_g, block + block // 2), bf16),
            jax.ShapeDtypeStruct((CHUNKS, cols, chunk), bf16),
        ),
        in_specs=[anywhere] * 5,
        out_specs=(anywhere,) * 3,
        scratch_shapes=scratch,
        compiler_params=pltpu.CompilerParams(
            collective_id=0, has_side_effects=True, vmem_limit_bytes=60 * 1024 * 1024
        ),
    )(activations, out_grads, grad_weight.T, basis_a, basis_g)
    inside = pl.BlockSpec(memory_space=pltpu.VMEM)
    factor_a, factor_g, precond = pl.pallas_call(
        functools.partial(finish, tokens, rows_a),
        out_shape=(
            jax.ShapeDtypeStruct((rows_a, block), f32),
            jax.ShapeDtypeStruct((rows_g, block), f32),
            jax.ShapeDtypeStruct((cols, rows), f32),
        ),
        in_specs=[inside] * 4,
        out_specs=(inside,) * 3,
        compiler_params=pltpu.CompilerParams(vmem_limit_bytes=60 * 1024 * 1024),
    )(here, there, back, basis_g)
    return factor_a, factor_g, precond.T


def solution(mesh):
    side = {64: 4, 16: 2}[mesh.shape["dp"]]
    in_specs = (P("dp", "mp"), P("dp", "mp"), P("mp", "dp"), P("mp", None), P("mp", None))
    out_specs = (P(("mp", "dp"), None), P(("mp", "dp"), None), P("mp", "dp"))
    return jax.shard_map(
        functools.partial(shards, side, side), mesh=mesh, in_specs=in_specs, out_specs=out_specs, check_vma=False
    )
```
